256 devices in a mesh: gx: 32 (over y, z), gy: 8 (over x, core).
Axes of the slice: x: 4, y: 4, z: 8, core: 2. Of those that a mesh axis runs over, the one named last changes fastest.
Arguments:
- tokens: bfloat16 [1, 512, 512, 128], P(None, 'gx', 'gy'), may hold values from -6 to 6
- norm_gain: float32 [128], replicated, may hold values from 0.1 to 1.9
- qkv_weight: bfloat16 [128, 384], replicated, may hold values from -0.5 to 0.5
- output_weight: bfloat16 [128, 128], replicated, may hold values from -0.5 to 0.5
- cotangent: bfloat16 [1, 512, 512, 128], P(None, 'gx', 'gy'), may hold values from -6 to 6
Outputs:
- block_output: bfloat16 [1, 512, 512, 128], P(None, 'gx', 'gy')
- token_grads: bfloat16 [1, 512, 512, 128], P(None, 'gx', 'gy')
- qkv_grads: float32 [128, 384], replicated
- output_grads: float32 [128, 128], replicated
- gain_grads: float32 [128], replicated
The draws below stay inside these ranges and needn't reach their ends.
All inputs are finite; a program needn't handle non-finite values.
Results may differ from the reference program's by a relative error of at most 0.0096.
Values may be sent and summed in bfloat16 or wider, within the bound.
A program may use at most 64 MiB of HBM per device.

```python
import jax
import jax.numpy as jnp
from jax import lax

C = 128
HEADS = 2
BATCH = 1
H = 512
W = 512


def level_of(key, shape, pieces, low, high):
    loudness = 1.0
    for axis_at, shards_of in pieces:
        steps = jax.random.uniform(jax.random.fold_in(jax.random.fold_in(key, 6), axis_at), (shards_of,), jnp.float32, low / len(pieces), high / len(pieces))
        loudness = loudness * jnp.repeat(jnp.exp(steps), shape[axis_at] // shards_of).reshape((-1,) + (1,) * (len(shape) - 1 - axis_at))
    return loudness


def centred(stream_key, extent, scale, reach, pieces=(), kind=jnp.bfloat16):
    drawn = jax.random.normal(stream_key, extent, jnp.float32) * scale
    if len(pieces) > 0:
        drawn = level_of(stream_key, extent, pieces, -0.22, 0.18) * drawn
    return jnp.clip(drawn, min=-reach, max=reach).astype(kind)


def setup_inputs(seed: int = 0) -> dict:
    key_list = jax.random.split(jax.random.key(seed), 6)
    tokens = centred(key_list[0], (BATCH, H, W, C), 1.0, 6.0, ((1, 32), (2, 8)))
    norm_gain = jnp.clip(1.0 + 0.18 * jax.random.normal(key_list[1], (C,), jnp.float32), 0.1, 1.9)
    qkv_weight = centred(key_list[2], (C, 3 * C), C ** -0.5, 0.5)
    output_weight = centred(key_list[3], (C, C), C ** -0.5, 0.5)
    cotangent = centred(key_list[4], (BATCH, H, W, C), 1.0, 6.0, ((1, 32), (2, 8)))
    return dict(tokens=tokens, norm_gain=norm_gain, qkv_weight=qkv_weight, output_weight=output_weight, cotangent=cotangent)


EPS = 1e-06

def to_blocks(values_in, tile_rows, tile_cols):
    features = values_in.shape[-1]
    shaped = values_in.reshape(tile_rows // 8, 8, tile_cols // 8, 8, features)
    return shaped.transpose(0, 2, 1, 3, 4).reshape(tile_rows // 8, tile_cols // 8, 64, features)

def from_blocks(blocks, tile_rows, tile_cols):
    features = blocks.shape[-1]
    shaped = blocks.reshape(tile_rows // 8, tile_cols // 8, 8, 8, features)
    return shaped.transpose(0, 2, 1, 3, 4).reshape(tile_rows, tile_cols, features)

def to_windows(values_in, tile_rows, tile_cols):
    features = values_in.shape[-1]
    block_rows = tile_rows // 8
    block_cols = tile_cols // 8
    upper_half = values_in[0:tile_rows].reshape(block_rows, 8, tile_cols + 8, features)
    lower_half = values_in[8:tile_rows + 8].reshape(block_rows, 8, tile_cols + 8, features)
    banded = jnp.concatenate([upper_half, lower_half], axis=1)
    left_half = banded[:, :, 0:tile_cols].reshape(block_rows, 16, block_cols, 8, features)
    right_half = banded[:, :, 8:tile_cols + 8].reshape(block_rows, 16, block_cols, 8, features)
    window_tiles = jnp.concatenate([left_half, right_half], axis=3)
    return window_tiles.transpose(0, 2, 1, 3, 4).reshape(block_rows, block_cols, 256, features)

def from_windows(window_tiles, tile_rows, tile_cols):
    features = window_tiles.shape[-1]
    block_rows = tile_rows // 8
    block_cols = tile_cols // 8
    shaped = window_tiles.reshape(block_rows, block_cols, 16, 16, features).transpose(0, 2, 1, 3, 4)
    left_half = shaped[:, :, :, 0:8].reshape(block_rows, 16, tile_cols, features)
    right_half = shaped[:, :, :, 8:16].reshape(block_rows, 16, tile_cols, features)
    banded = jnp.pad(left_half, ((0, 0), (0, 0), (0, 8), (0, 0))) + jnp.pad(right_half, ((0, 0), (0, 0), (8, 0), (0, 0)))
    upper_half = banded[:, 0:8].reshape(tile_rows, tile_cols + 8, features)
    lower_half = banded[:, 8:16].reshape(tile_rows, tile_cols + 8, features)
    return jnp.pad(upper_half, ((0, 8), (0, 0), (0, 0))) + jnp.pad(lower_half, ((8, 0), (0, 0), (0, 0)))

def window_mask(tile_rows, tile_cols, row_start, col_start, image_height, image_width):
    centre = jnp.arange(64, dtype=jnp.int32)
    beside_all = jnp.arange(256, dtype=jnp.int32)
    row_gap = beside_all[None, :] // 16 - centre[:, None] // 8
    col_gap = beside_all[None, :] % 16 - centre[:, None] % 8
    near_mask = ((row_gap >= 1) & (row_gap <= 7) & (col_gap >= 1) & (col_gap <= 7)).astype(jnp.float32)
    global_row = row_start - 4 + jnp.arange(tile_rows // 8, dtype=jnp.int32)[:, None] * 8 + beside_all[None, :] // 16
    global_col = col_start - 4 + jnp.arange(tile_cols // 8, dtype=jnp.int32)[:, None] * 8 + beside_all[None, :] % 16
    row_inside = ((global_row >= 0) & (global_row < image_height)).astype(jnp.float32)
    col_inside = ((global_col >= 0) & (global_col < image_width)).astype(jnp.float32)
    inside = row_inside[:, None, :] * col_inside[None, :, :]
    return (near_mask[None, None] * inside[:, :, None, :], inside)

def split_heads(values_in, head_count):
    return values_in.reshape(values_in.shape[:-1] + (head_count, values_in.shape[-1] // head_count))

def query_side(query, keyval, d_attended, window_on, tile_rows, tile_cols, head_count):
    channels = query.shape[-1]
    block_rows = tile_rows // 8
    block_cols = tile_cols // 8
    query_blocks = split_heads(to_blocks(query, tile_rows, tile_cols), head_count).astype(jnp.float32)
    windows = to_windows(keyval, tile_rows, tile_cols)
    key_windows = split_heads(windows[..., :channels], head_count).astype(jnp.float32)
    value_windows = split_heads(windows[..., channels:], head_count).astype(jnp.float32)
    scores = jnp.einsum('xyqhd,xykhd->xyhqk', query_blocks, key_windows)
    weights = jnp.exp(scores) * window_on[:, :, None]
    totals = lax.optimization_barrier(jnp.sum(weights, axis=-1))
    shares = weights / totals[..., None]
    shares_low = lax.optimization_barrier(shares.astype(jnp.bfloat16))
    attended = jnp.einsum('xyhqk,xykhd->xyqhd', shares_low.astype(jnp.float32), value_windows)
    grad_blocks = split_heads(to_blocks(d_attended, tile_rows, tile_cols), head_count).astype(jnp.float32)
    d_shares = jnp.einsum('xyqhd,xykhd->xyhqk', grad_blocks, value_windows)
    delta_sum = lax.optimization_barrier(jnp.sum(shares * d_shares, axis=-1))
    d_scores = lax.optimization_barrier((shares * (d_shares - delta_sum[..., None])).astype(jnp.bfloat16))
    d_scores = d_scores.astype(jnp.float32)
    d_query = jnp.einsum('xyhqk,xykhd->xyqhd', d_scores, key_windows)
    d_key = jnp.einsum('xyhqk,xyqhd->xykhd', d_scores, query_blocks)
    d_value = jnp.einsum('xyhqk,xyqhd->xykhd', shares_low.astype(jnp.float32), grad_blocks)
    attended = from_blocks(attended.reshape(block_rows, block_cols, 64, channels), tile_rows, tile_cols).astype(jnp.bfloat16)
    d_query = from_blocks(d_query.reshape(block_rows, block_cols, 64, channels), tile_rows, tile_cols)
    joined = jnp.concatenate([d_key.reshape(block_rows, block_cols, 256, channels), d_value.reshape(block_rows, block_cols, 256, channels)], axis=-1)
    return (attended, d_query, from_windows(joined, tile_rows, tile_cols))

def image_pass(query, keyval, d_attended):
    image_height, image_width, channels = query.shape
    padded = jnp.pad(keyval, ((4, 4), (4, 4), (0, 0)))

    def band(carried, band_index):
        row_start = band_index * 8
        query_band = lax.dynamic_slice_in_dim(query, row_start, 8, 0)
        key_band = lax.dynamic_slice_in_dim(padded, row_start, 16, 0)
        grad_band = lax.dynamic_slice_in_dim(d_attended, row_start, 8, 0)
        window_on, inside = window_mask(8, image_width, row_start, 0, image_height, image_width)
        attended, d_query, d_keyval = query_side(query_band, key_band, grad_band, window_on, 8, image_width, HEADS)
        return (carried, (attended, d_query, d_keyval[0:8], d_keyval[8:16]))
    carried, outputs = lax.scan(band, jnp.zeros((), jnp.float32), jnp.arange(image_height // 8, dtype=jnp.int32))
    attended, d_query, upper_half, lower_half = outputs
    features = upper_half.shape[-1]
    upper_half = upper_half.reshape(image_height, image_width + 8, features)
    lower_half = lower_half.reshape(image_height, image_width + 8, features)
    spread = jnp.pad(upper_half, ((0, 8), (0, 0), (0, 0))) + jnp.pad(lower_half, ((8, 0), (0, 0), (0, 0)))
    d_keyval = spread[4:image_height + 4, 4:image_width + 4]
    q_scale = (channels // HEADS) ** (-0.5)
    d_query = d_query.reshape(image_height, image_width, channels) * q_scale
    d_projected = jnp.concatenate([d_query, d_keyval], axis=-1).astype(jnp.bfloat16)
    return (attended.reshape(image_height, image_width, channels), d_projected)

def per_image(image_items):
    return image_pass(image_items[0], image_items[1], image_items[2])

def reference(tokens, norm_gain, qkv_weight, output_weight, cotangent):
    q_scale = (C // HEADS) ** (-0.5)
    flat_tokens = tokens.reshape(-1, C).astype(jnp.float32)
    flat_grads = cotangent.reshape(-1, C)
    inverse_rms = lax.rsqrt(lax.optimization_barrier(jnp.mean(flat_tokens * flat_tokens, axis=-1, keepdims=True)) + EPS)
    unit_rows = flat_tokens * inverse_rms
    normed = (unit_rows * norm_gain).astype(jnp.bfloat16)
    projected = jnp.dot(normed, qkv_weight, preferred_element_type=jnp.float32)
    query = lax.optimization_barrier((projected[:, :C] * q_scale).astype(jnp.bfloat16)).reshape(BATCH, H, W, C)
    keyval = lax.optimization_barrier(projected[:, C:].astype(jnp.bfloat16)).reshape(BATCH, H, W, 2 * C)
    d_attended = lax.dot_general(flat_grads, output_weight, (((1,), (1,)), ((), ())), preferred_element_type=jnp.float32)
    d_attended = lax.optimization_barrier(d_attended.astype(jnp.bfloat16)).reshape(BATCH, H, W, C)
    attended, d_projected = lax.map(per_image, (query, keyval, d_attended))
    flat_attended = attended.reshape(-1, C)
    mixed_rows = flat_tokens + jnp.dot(flat_attended, output_weight, preferred_element_type=jnp.float32)
    block_output = mixed_rows.astype(jnp.bfloat16).reshape(tokens.shape)
    d_projected = d_projected.reshape(-1, 3 * C)
    d_normed = lax.dot_general(d_projected, qkv_weight, (((1,), (1,)), ((), ())), preferred_element_type=jnp.float32)
    scaled_grad = d_normed * norm_gain
    d_flat = flat_grads.astype(jnp.float32) + inverse_rms * (scaled_grad - unit_rows * lax.optimization_barrier(jnp.mean(scaled_grad * unit_rows, axis=-1, keepdims=True)))
    factor = (BATCH * H * W) ** (-0.5)
    qkv_grads = lax.dot_general(normed, d_projected, (((0,), (0,)), ((), ())), preferred_element_type=jnp.float32) * factor
    output_grads = lax.dot_general(flat_attended, flat_grads, (((0,), (0,)), ((), ())), preferred_element_type=jnp.float32) * factor
    gain_grads = lax.optimization_barrier(jnp.sum(d_normed * unit_rows, axis=0)) * factor
    token_grads = d_flat.astype(jnp.bfloat16).reshape(tokens.shape)
    return (block_output, token_grads, qkv_grads, output_grads, gain_grads)
```

```python
import functools

import jax
import jax.numpy as jnp
from jax import lax
from jax.experimental import pallas as pl
from jax.experimental.pallas import tpu as pltpu
from jax.sharding import PartitionSpec as P

MESH = pl.DeviceIdType.MESH
EPS = 1e-06
F32 = jnp.float32
BF16 = jnp.bfloat16
C = 128
RL, CL = 16, 64
RE, CE = RL + 6, CL + 8
NB = CL // 8
KEYS = RE * 16
NEG = -1e30
ZN = 8

NT = (((1,), (1,)), ((), ()))
TN = (((0,), (0,)), ((), ()))


def dot(a, b, dims=(((1,), (0,)), ((), ()))):
    return lax.dot_general(a, b, dims, preferred_element_type=F32)


def inverse_rms(x):
    return lax.rsqrt(jnp.sum(x * x, axis=-1, keepdims=True) * (1.0 / C) + EPS)


def kernel(
    gxn, gyn, zn,
    tok, gain, wqkv, wout, cot,
    out, tgrad, qkvg, outg, gaing,
    rx_rows, rx_cols, rx_corner,
    x_ext, u_ext, k_ext, v_ext, dk_ext, dv_ext,
    q2, da2, att, dq, near,
    tx2_rows, tx2_cols, tx2_corner, rx2_rows, rx2_cols, rx2_corner,
    gsum, g16, rs_rx, z_rx, ag,
    h_send, h_recv, d_send, d_recv, a_send, a_recv,
):
    yn = gxn // zn
    na = yn * gyn
    rows = 512 // na
    gx = lax.axis_index("gx")
    gy = lax.axis_index("gy")
    y, z = gx // zn, gx % zn
    me = y * gyn + gy

    def beside(dr, dc):
        return ((gx + dr + gxn) % gxn, (gy + dc + gyn) % gyn)

    def plane(d):
        m = (me + d) % na
        return m, ((m // gyn) * zn + z, m % gyn)

    def column(d):
        return (y * zn + (z + d) % zn, gy)

    around = [(dr, dc) for dr in (-1, 0, 1) for dc in (-1, 0, 1) if dr or dc]
    barrier = pltpu.get_barrier_semaphore()
    for dr, dc in around:
        pl.semaphore_signal(barrier, inc=1, device_id=beside(dr, dc), device_id_type=MESH)
    for d in range(1, zn):
        pl.semaphore_signal(barrier, inc=1, device_id=column(d), device_id_type=MESH)
    for d in range(1, na):
        pl.semaphore_signal(barrier, inc=1, device_id=plane(d)[1], device_id_type=MESH)

    lane = lax.broadcasted_iota(jnp.int32, (1, C), 1)
    head0 = lane < 64

    def two_heads(v):
        v = v.astype(BF16)
        zero = jnp.zeros_like(v)
        return jnp.concatenate([jnp.where(head0, v, zero), jnp.where(head0, zero, v)], axis=0)

    x = tok[...].astype(F32).reshape(RL * CL, C)
    x_ext[3 : RL + 3, 4 : CL + 4, :] = x.reshape(RL, CL, C)
    unit = x * inverse_rms(x)
    normed = (unit * gain[...]).astype(BF16)
    query = (dot(normed, wqkv[:, 0:C]) * 0.125).reshape(RL, CL, C)
    d_att = dot(cot[...].reshape(RL * CL, C), wout[...], NT).reshape(RL, CL, C)
    for j in range(NB):
        q2[j] = two_heads(query[:, 8 * j : 8 * j + 8, :].reshape(RL * 8, C))
        da2[j] = two_heads(d_att[:, 8 * j : 8 * j + 8, :].reshape(RL * 8, C))

    key_at = lax.broadcasted_iota(jnp.int32, (RE, 16, 256), 0)
    key_col = lax.broadcasted_iota(jnp.int32, (RE, 16, 256), 1)
    at = lax.broadcasted_iota(jnp.int32, (RE, 16, 256), 2)
    q_row = (at // 8) % RL
    q_col = at % 8
    image_row = gx * RL + key_at - 3
    ok = (
        (key_at >= q_row) & (key_at <= q_row + 6)
        & (key_col >= q_col + 1) & (key_col <= q_col + 7)
        & (image_row >= 0) & (image_row < gxn * RL)
    )
    near[...] = jnp.where(ok, 0.0, NEG)
    dk_ext[...] = jnp.zeros_like(dk_ext)
    dv_ext[...] = jnp.zeros_like(dv_ext)

    pl.semaphore_wait(barrier, 8 + (zn - 1) + (na - 1))

    copies = []
    for i, (dr, dc) in enumerate(around):
        rsl = slice(0, RL) if dr == 0 else (slice(0, 3) if dr < 0 else slice(RL - 3, RL))
        csl = slice(0, CL) if dc == 0 else (slice(0, 16) if dc < 0 else slice(CL - 16, CL))
        src = tok.at[rsl, csl]
        if dc == 0:
            dst = rx_rows.at[0 if dr > 0 else 1]
        elif dr == 0:
            dst = rx_cols.at[0 if dc > 0 else 1]
        else:
            dst = rx_corner.at[(0 if dr > 0 else 2) + (0 if dc > 0 else 1)]
        copy = pltpu.make_async_remote_copy(
            src, dst, h_send.at[i], h_recv.at[i], device_id=beside(dr, dc), device_id_type=MESH
        )
        copy.start()
        copies.append(copy)
    for copy in copies:
        copy.wait()

    x_ext[0:3, 4 : CL + 4, :] = rx_rows[0].astype(F32)
    x_ext[RL + 3 : RE, 4 : CL + 4, :] = rx_rows[1].astype(F32)
    x_ext[3 : RL + 3, 0:4, :] = rx_cols[0].astype(F32)[:, 12:16]
    x_ext[3 : RL + 3, CL + 4 : CE, :] = rx_cols[1].astype(F32)[:, 0:4]
    x_ext[0:3, 0:4, :] = rx_corner[0].astype(F32)[:, 12:16]
    x_ext[0:3, CL + 4 : CE, :] = rx_corner[1].astype(F32)[:, 0:4]
    x_ext[RL + 3 : RE, 0:4, :] = rx_corner[2].astype(F32)[:, 12:16]
    x_ext[RL + 3 : RE, CL + 4 : CE, :] = rx_corner[3].astype(F32)[:, 0:4]
    xe = x_ext[...].reshape(RE * CE, C)
    ue = xe * inverse_rms(xe)
    u_ext[...] = ue.astype(BF16)
    keyval = dot((ue * gain[...]).astype(BF16), wqkv[:, C : 3 * C])
    k_ext[...] = keyval[:, 0:C].reshape(RE, CE, C)
    v_ext[...] = keyval[:, C : 2 * C].reshape(RE, CE, C)

    def block(j, carry):
        j0 = pl.multiple_of(j * 8, 8)
        window = pl.ds(j0, 16)
        kw = k_ext[:, window, :].reshape(KEYS, C).astype(BF16)
        vw = v_ext[:, window, :].reshape(KEYS, C).astype(BF16)
        qb, db = q2[j], da2[j]
        scores = dot(kw, qb, NT).reshape(RE, 16, 256)
        image_col = gy * CL + j0 - 4 + lax.broadcasted_iota(jnp.int32, (1, 16, 256), 1)
        edge = jnp.where((image_col >= 0) & (image_col < gyn * CL), 0.0, NEG)
        weights = jnp.exp(scores + near[...] + edge).reshape(KEYS, 256)
        totals = jnp.sum(weights, axis=0, keepdims=True)
        shares = weights * (1.0 / totals)
        shares_low = shares.astype(BF16)
        d_shares = dot(vw, db, NT)
        delta = jnp.sum(shares * d_shares, axis=0, keepdims=True)
        d_scores = (shares * (d_shares - delta)).astype(BF16)
        a2 = dot(shares_low, vw, TN)
        dq2 = dot(d_scores, kw, TN)
        own = pl.ds(j0, 8)
        att[:, own, :] = jnp.where(head0, a2[0:128], a2[128:256]).reshape(RL, 8, C)
        dq[:, own, :] = jnp.where(head0, dq2[0:128], dq2[128:256]).reshape(RL, 8, C)
        dk_ext[:, window, :] += dot(d_scores, qb).reshape(RE, 16, C)
        dv_ext[:, window, :] += dot(shares_low, db).reshape(RE, 16, C)
        return carry

    lax.fori_loop(0, NB, block, 0)

    attended = att[...].reshape(RL * CL, C).astype(BF16)
    d_query = (dq[...] * 0.125).reshape(RL * CL, C).astype(BF16)
    cot_rows = cot[...].reshape(RL * CL, C)
    u = u_ext[...]
    gsum[0:C, :] = dot(unit.astype(BF16), d_query, TN)
    gsum[C : 2 * C, :] = dot(u, dk_ext[...].reshape(RE * CE, C).astype(BF16), TN)
    gsum[2 * C : 3 * C, :] = dot(u, dv_ext[...].reshape(RE * CE, C).astype(BF16), TN)
    gsum[3 * C : 4 * C, :] = dot(attended, cot_rows, TN)
    g16[...] = gsum[...].astype(BF16)
    for d in range(1, na):
        m, device = plane(d)
        pltpu.make_async_remote_copy(
            g16.at[pl.ds(pl.multiple_of(m * rows, rows), rows)],
            rs_rx.at[pl.ds((d - 1) * rows, rows)],
            a_send.at[0], a_recv.at[0], device_id=device, device_id_type=MESH,
        ).start()

    both = jnp.concatenate([dk_ext[...], dv_ext[...]], axis=-1)
    pad_rows = jnp.zeros((8, 2 * C), F32)
    for i, lo in enumerate((0, RL + 3)):
        flat = both[lo : lo + 3].reshape(3 * CE, 2 * C)
        tx2_rows[i] = jnp.concatenate([flat, pad_rows], axis=0).astype(BF16)
        for k, left in enumerate((0, CL)):
            corner = both[lo : lo + 3, left : left + 8].reshape(24, 2 * C)
            tx2_corner[2 * i + k] = jnp.concatenate([corner, pad_rows], axis=0).astype(BF16)
    for k, left in enumerate((0, CL)):
        tx2_cols[k] = both[3 : RL + 3, left : left + 8].reshape(RL * 8, 2 * C).astype(BF16)
    back = []
    for i, (dr, dc) in enumerate(around):
        if dc == 0:
            n = 0 if dr < 0 else 1
            src, dst = tx2_rows.at[n], rx2_rows.at[n]
        elif dr == 0:
            n = 0 if dc < 0 else 1
            src, dst = tx2_cols.at[n], rx2_cols.at[n]
        else:
            n = (0 if dr < 0 else 2) + (0 if dc < 0 else 1)
            src, dst = tx2_corner.at[n], rx2_corner.at[n]
        copy = pltpu.make_async_remote_copy(
            src, dst, d_send.at[i], d_recv.at[i], device_id=beside(dr, dc), device_id_type=MESH
        )
        copy.start()
        back.append(copy)

    out[...] = (x + dot(attended, wout[...])).astype(BF16).reshape(RL, CL, C)

    def wait_bytes(ref, sem):
        pltpu.make_async_copy(ref, ref, sem).wait()

    wait_bytes(rs_rx, a_recv.at[0])
    mine = gsum[pl.ds(pl.multiple_of(me * rows, rows), rows), :]
    parts = rs_rx[...].astype(F32).reshape(na - 1, rows, C)
    z_rx[pl.ds(z, 1)] = (mine + jnp.sum(parts, axis=0)).astype(BF16)[None]
    for d in range(1, zn):
        pltpu.make_async_remote_copy(
            z_rx.at[z], z_rx.at[z],
            a_send.at[1], a_recv.at[1], device_id=column(d), device_id_type=MESH,
        ).start()

    for copy in back:
        copy.wait()
    sub = lax.broadcasted_iota(jnp.int32, (1, 8, 1), 1)
    tile = lax.broadcasted_iota(jnp.int32, (1, CE, 1), 1)
    inner = (tile >= 4) & (tile < CL + 4)

    def add(rsl, csl, rx, n, mask):
        shape = (rsl.stop - rsl.start, csl.stop - csl.start, 2 * C)
        add_rows = rx[n].astype(F32)[0 : shape[0] * shape[1]].reshape(shape)
        add_rows = jnp.where(mask, add_rows, 0.0)
        dk_ext[rsl, csl, :] += add_rows[:, :, 0:C]
        dv_ext[rsl, csl, :] += add_rows[:, :, C : 2 * C]

    first, last = slice(3, 6), slice(RL, RL + 3)
    left, right = slice(0, 8), slice(CL, CE)
    add(last, slice(0, CE), rx2_rows, 0, inner)
    add(first, slice(0, CE), rx2_rows, 1, inner)
    add(slice(3, RL + 3), right, rx2_cols, 0, sub < 4)
    add(slice(3, RL + 3), left, rx2_cols, 1, sub >= 4)
    add(last, right, rx2_corner, 0, sub < 4)
    add(last, left, rx2_corner, 1, sub >= 4)
    add(first, right, rx2_corner, 2, sub < 4)
    add(first, left, rx2_corner, 3, sub >= 4)
    d_key = dk_ext[3 : RL + 3, 4 : CL + 4, :].reshape(RL * CL, C).astype(BF16)
    d_value = dv_ext[3 : RL + 3, 4 : CL + 4, :].reshape(RL * CL, C).astype(BF16)
    d_normed = (
        dot(d_query, wqkv[:, 0:C], NT)
        + dot(d_key, wqkv[:, C : 2 * C], NT)
        + dot(d_value, wqkv[:, 2 * C : 3 * C], NT)
    )
    x = tok[...].astype(F32).reshape(RL * CL, C)
    r = inverse_rms(x)
    unit = x * r
    g = d_normed * gain[...]
    mean = jnp.sum(g * unit, axis=-1, keepdims=True) * (1.0 / C)
    grads = cot_rows.astype(F32) + r * (g - unit * mean)
    tgrad[...] = grads.astype(BF16).reshape(RL, CL, C)

    wait_bytes(z_rx.at[pl.ds(0, zn - 1)], a_recv.at[1])
    wait_bytes(z_rx.at[pl.ds(0, zn - 1)], a_send.at[1])
    here = pl.ds(pl.multiple_of(me * rows, rows), rows)
    ag[here, :] = jnp.sum(z_rx[...].astype(F32), axis=0).astype(BF16)
    for d in range(1, na):
        m, device = plane(d)
        pltpu.make_async_remote_copy(
            ag.at[here], ag.at[here],
            a_send.at[2], a_recv.at[2], device_id=device, device_id_type=MESH,
        ).start()
    wait_bytes(rs_rx, a_send.at[0])
    wait_bytes(rs_rx, a_recv.at[2])
    wait_bytes(rs_rx, a_send.at[2])
    factor = (gxn * RL * gyn * CL) ** (-0.5)
    eye = lax.broadcasted_iota(jnp.int32, (C, C), 0) == lax.broadcasted_iota(jnp.int32, (C, C), 1)
    gain_col = jnp.sum(jnp.where(eye, gain[...], 0.0), axis=1, keepdims=True)
    total = jnp.zeros((C, C), F32)
    for i in range(3):
        piece = ag[i * C : (i + 1) * C, :].astype(F32) * factor
        qkvg[:, i * C : (i + 1) * C] = piece * gain_col
        total += piece * wqkv[:, i * C : (i + 1) * C].astype(F32)
    outg[...] = ag[3 * C : 4 * C, :].astype(F32) * factor
    gain_sum = jnp.sum(total, axis=1, keepdims=True)
    gaing[...] = jnp.sum(jnp.where(eye, gain_sum, 0.0), axis=0, keepdims=True)


def per_device(gxn, gyn, zn, tokens, norm_gain, qkv_weight, output_weight, cotangent):
    na = (gxn // zn) * gyn
    rows = 512 // na
    vmem = pl.BlockSpec(memory_space=pltpu.VMEM)
    sds = jax.ShapeDtypeStruct
    outs = pl.pallas_call(
        functools.partial(kernel, gxn, gyn, zn),
        out_shape=(
            sds((RL, CL, C), BF16),
            sds((RL, CL, C), BF16),
            sds((C, 3 * C), F32),
            sds((C, C), F32),
            sds((1, C), F32),
        ),
        in_specs=[vmem] * 5,
        out_specs=(vmem,) * 5,
        scratch_shapes=[
            pltpu.VMEM((2, 3, CL, C), BF16),
            pltpu.VMEM((2, RL, 16, C), BF16),
            pltpu.VMEM((4, 3, 16, C), BF16),
            pltpu.VMEM((RE, CE, C), F32),
            pltpu.VMEM((RE * CE, C), BF16),
            pltpu.VMEM((RE, CE, C), F32),
            pltpu.VMEM((RE, CE, C), F32),
            pltpu.VMEM((RE, CE, C), F32),
            pltpu.VMEM((RE, CE, C), F32),
            pltpu.VMEM((NB, 256, C), BF16),
            pltpu.VMEM((NB, 256, C), BF16),
            pltpu.VMEM((RL, CL, C), F32),
            pltpu.VMEM((RL, CL, C), F32),
            pltpu.VMEM((RE, 16, 256), F32),
            pltpu.VMEM((2, 224, 2 * C), BF16),
            pltpu.VMEM((2, RL * 8, 2 * C), BF16),
            pltpu.VMEM((4, 32, 2 * C), BF16),
            pltpu.VMEM((2, 224, 2 * C), BF16),
            pltpu.VMEM((2, RL * 8, 2 * C), BF16),
            pltpu.VMEM((4, 32, 2 * C), BF16),
            pltpu.VMEM((4 * C, C), F32),
            pltpu.VMEM((4 * C, C), BF16),
            pltpu.VMEM(((na - 1) * rows, C), BF16),
            pltpu.VMEM((zn, rows, C), BF16),
            pltpu.VMEM((4 * C, C), BF16),
            pltpu.SemaphoreType.DMA((8,)),
            pltpu.SemaphoreType.DMA((8,)),
            pltpu.SemaphoreType.DMA((8,)),
            pltpu.SemaphoreType.DMA((8,)),
            pltpu.SemaphoreType.DMA((3,)),
            pltpu.SemaphoreType.DMA((3,)),
        ],
        compiler_params=pltpu.CompilerParams(
            collective_id=0, has_side_effects=True, vmem_limit_bytes=40 << 20
        ),
    )(
        tokens.reshape(RL, CL, C),
        norm_gain.reshape(1, C),
        qkv_weight,
        output_weight,
        cotangent.reshape(RL, CL, C),
    )
    out, tgrad, qkvg, outg, gaing = outs
    return (
        out.reshape(tokens.shape),
        tgrad.reshape(tokens.shape),
        qkvg,
        outg,
        gaing.reshape(C),
    )


def solution(mesh):
    gxn, gyn = mesh.shape["gx"], mesh.shape["gy"]
    image = P(None, "gx", "gy", None)
    return jax.shard_map(
        functools.partial(per_device, gxn, gyn, min(ZN, max(gxn // 4, 2))),
        mesh=mesh,
        in_specs=(image, P(), P(), P(), image),
        out_specs=(image, image, P(), P(), P()),
        check_vma=False,
    )
```

```python
import functools

import jax
import jax.numpy as jnp
from jax import lax
from jax.experimental import pallas as pl
from jax.experimental.pallas import tpu as pltpu
from jax.sharding import PartitionSpec as P

MESH = pl.DeviceIdType.MESH
EPS = 1e-06
F32 = jnp.float32
BF16 = jnp.bfloat16
C = 128
RL, CL = 16, 64
RE, CE = RL + 6, CL + 8
NB = CL // 8
STRIP = 32
INNER_UNROLL = 6
STRIP_UNROLL = 2
NEG = -1e30
ZN = 8

NT = (((1,), (1,)), ((), ()))
TN = (((0,), (0,)), ((), ()))


def dot(a, b, dims=(((1,), (0,)), ((), ()))):
    return lax.dot_general(a, b, dims, preferred_element_type=F32)


def inverse_rms(x):
    return lax.rsqrt(jnp.sum(x * x, axis=-1, keepdims=True) * (1.0 / C) + EPS)


def kernel(
    gxn, gyn, zn,
    tok_hbm, gain_hbm, wqkv_hbm, wout_hbm, cot_hbm,
    out_hbm, tgrad_hbm, qkvg_hbm, outg_hbm, gaing_hbm,
    tok, gain, wqkv, wout, cot,
    out, tgrad, qkvg, outg, gaing,
    rx_rows, rx_cols, rx_corner,
    u_ext, k_ext, v_ext, dk_ext, dv_ext, dn_ext,
    q_loc, da_loc, att, dq,
    tx2_rows, tx2_cols, tx2_corner, rx2_rows, rx2_cols, rx2_corner,
    gsum, g16, rs_rx, z_rx, ag,
    in_sem, out_sem, h_send, h_recv, d_send, d_recv, a_send, a_recv,
):
    yn = gxn // zn
    na = yn * gyn
    rows = 512 // na
    gx = lax.axis_index("gx")
    gy = lax.axis_index("gy")
    y, z = gx // zn, gx % zn
    me = y * gyn + gy

    def beside(dr, dc):
        return ((gx + dr + gxn) % gxn, (gy + dc + gyn) % gyn)

    def exists(dr, dc):
        r, c = gx + dr, gy + dc
        return (r >= 0) & (r < gxn) & (c >= 0) & (c < gyn)

    def plane(d):
        m = (me + d) % na
        return m, ((m // gyn) * zn + z, m % gyn)

    def column(d):
        return (y * zn + (z + d) % zn, gy)

    def wait_bytes(ref, sem):
        pltpu.make_async_copy(ref, ref, sem).wait()

    around = [(dr, dc) for dr in (-1, 0, 1) for dc in (-1, 0, 1) if dr or dc]
    barrier = pltpu.get_barrier_semaphore()

    def greet(device):
        pl.semaphore_signal(barrier, inc=1, device_id=device, device_id_type=MESH)

    for dr, dc in around:
        if dr:
            greet(beside(dr, dc))
    for d in range(1, zn):
        greet(column(d))
    for d in range(1, na):
        greet(plane(d)[1])

    fetches = [
        pltpu.make_async_copy(src, dst, in_sem.at[i])
        for i, (src, dst) in enumerate(
            ((tok_hbm, tok), (gain_hbm, gain), (wqkv_hbm, wqkv), (cot_hbm, cot), (wout_hbm, wout))
        )
    ]
    for fetch in fetches:
        fetch.start()

    pl.semaphore_wait(barrier, 6 + (zn - 1) + (na - 1))

    halo = []
    for i, (dr, dc) in enumerate(around):
        rsl = slice(0, RL) if dr == 0 else (slice(0, 3) if dr < 0 else slice(RL - 3, RL))
        csl = slice(0, CL) if dc == 0 else (slice(0, 16) if dc < 0 else slice(CL - 16, CL))
        src = tok_hbm.at[rsl, csl]
        if dc == 0:
            dst = rx_rows.at[0 if dr > 0 else 1]
        elif dr == 0:
            dst = rx_cols.at[0 if dc > 0 else 1]
        else:
            dst = rx_corner.at[(0 if dr > 0 else 2) + (0 if dc > 0 else 1)]
        copy = pltpu.make_async_remote_copy(
            src, dst, h_send.at[i], h_recv.at[i], device_id=beside(dr, dc), device_id_type=MESH
        )
        halo.append((copy, dst, exists(dr, dc), exists(-dr, -dc)))
    for copy, dst, to, _ in halo:
        pl.when(to)(copy.start)

    for fetch in fetches:
        fetch.wait()
    dk_ext[...] = jnp.zeros_like(dk_ext)
    dv_ext[...] = jnp.zeros_like(dv_ext)
    u_ext[...] = jnp.zeros_like(u_ext)
    gains = gain[...]

    def keyval(unit):
        return dot((unit * gains).astype(BF16), wqkv[:, C : 3 * C])

    x = tok[...].astype(F32).reshape(RL * CL, C)
    unit = x * inverse_rms(x)
    normed = (unit * gains).astype(BF16)
    u_ext[3 : RL + 3, 4 : CL + 4, :] = unit.reshape(RL, CL, C)
    projected = dot(normed, wqkv[...])
    q_loc[...] = (projected[:, 0:C] * 0.125).reshape(RL, CL, C)
    k_ext[3 : RL + 3, 4 : CL + 4, :] = projected[:, C : 2 * C].reshape(RL, CL, C)
    v_ext[3 : RL + 3, 4 : CL + 4, :] = projected[:, 2 * C : 3 * C].reshape(RL, CL, C)
    da_loc[...] = dot(cot[...].reshape(RL * CL, C), wout[...], NT).reshape(RL, CL, C)

    head0 = lax.broadcasted_iota(jnp.int32, (1, C), 1) < 64

    def two_heads(v):
        v = v.astype(BF16)
        zero = jnp.zeros_like(v)
        return jnp.concatenate([jnp.where(head0, v, zero), jnp.where(head0, zero, v)], axis=0)

    def block(row0, nr, col0, nc):
        kr, kc, nq = nr + 6, nc + 8, nr * nc
        lanes = 2 * nq
        keys = (slice(row0, row0 + kr), pl.ds(col0, kc))
        own = (slice(row0, row0 + nr), pl.ds(col0, nc))
        at = lax.broadcasted_iota(jnp.int32, (1, 1, lanes), 2) % nq
        q_row, q_col = at // nc, at % nc
        key_row = lax.broadcasted_iota(jnp.int32, (kr, 1, lanes), 0)
        key_col = lax.broadcasted_iota(jnp.int32, (1, kc, lanes), 1)
        image_row = gx * RL + row0 - 3 + key_row
        image_col = gy * CL + col0 - 4 + key_col
        row_bias = jnp.where(
            (key_row >= q_row) & (key_row <= q_row + 6) & (image_row >= 0) & (image_row < gxn * RL), 0.0, NEG
        )
        col_bias = jnp.where(
            (key_col >= q_col + 1) & (key_col <= q_col + 7) & (image_col >= 0) & (image_col < gyn * CL), 0.0, NEG
        )
        kw = k_ext[keys[0], keys[1], :].reshape(kr * kc, C).astype(BF16)
        vw = v_ext[keys[0], keys[1], :].reshape(kr * kc, C).astype(BF16)
        qb = two_heads(q_loc[own[0], own[1], :].reshape(nq, C))
        db = two_heads(da_loc[own[0], own[1], :].reshape(nq, C))
        scores = dot(kw, qb, NT).reshape(kr, kc, lanes)
        weights = jnp.exp(scores + row_bias + col_bias).reshape(kr * kc, lanes)
        totals = jnp.sum(weights, axis=0, keepdims=True)
        shares = weights * (1.0 / totals)
        shares_low = shares.astype(BF16)
        d_shares = dot(vw, db, NT)
        delta = jnp.sum(shares * d_shares, axis=0, keepdims=True)
        d_scores = (shares * (d_shares - delta)).astype(BF16)
        a2 = dot(shares_low, vw, TN)
        dq2 = dot(d_scores, kw, TN)
        att[own[0], own[1], :] = jnp.where(head0, a2[0:nq], a2[nq:]).reshape(nr, nc, C)
        dq[own[0], own[1], :] = jnp.where(head0, dq2[0:nq], dq2[nq:]).reshape(nr, nc, C)
        dk_ext[keys[0], keys[1], :] += dot(d_scores, qb).reshape(kr, kc, C)
        dv_ext[keys[0], keys[1], :] += dot(shares_low, db).reshape(kr, kc, C)

    def inner(j, carry):
        block(3, RL - 6, pl.multiple_of(j * 8, 8), 8)
        return carry

    lax.fori_loop(1, NB - 1, inner, 0, unroll=INNER_UNROLL)

    for copy, dst, _, come in halo:
        pl.when(come)(copy.wait_recv)

        @pl.when(jnp.logical_not(come))
        def _():
            dst[...] = jnp.zeros(dst.shape, BF16)

    rims = (
        (rx_rows[0].astype(F32), slice(0, 3), slice(4, CL + 4), slice(0, CL)),
        (rx_rows[1].astype(F32), slice(RL + 3, RE), slice(4, CL + 4), slice(0, CL)),
        (rx_cols[0].astype(F32)[:, 8:16], slice(3, RL + 3), slice(0, 4), slice(4, 8)),
        (rx_cols[1].astype(F32)[:, 0:8], slice(3, RL + 3), slice(CL + 4, CE), slice(0, 4)),
        (rx_corner[0].astype(F32)[:, 8:16], slice(0, 3), slice(0, 4), slice(4, 8)),
        (rx_corner[1].astype(F32)[:, 0:8], slice(0, 3), slice(CL + 4, CE), slice(0, 4)),
        (rx_corner[2].astype(F32)[:, 8:16], slice(RL + 3, RE), slice(0, 4), slice(4, 8)),
        (rx_corner[3].astype(F32)[:, 0:8], slice(RL + 3, RE), slice(CL + 4, CE), slice(0, 4)),
    )
    xh = jnp.concatenate([rim[0].reshape(-1, C) for rim in rims], axis=0)
    uh = xh * inverse_rms(xh)
    kvh = keyval(uh)
    start = 0
    for tokens, rsl, csl, used in rims:
        shape = tokens.shape
        n = shape[0] * shape[1]
        u_ext[rsl, csl, :] = uh[start : start + n].reshape(shape)[:, used]
        k_ext[rsl, csl, :] = kvh[start : start + n, 0:C].reshape(shape)[:, used]
        v_ext[rsl, csl, :] = kvh[start : start + n, C : 2 * C].reshape(shape)[:, used]
        start += n

    block(3, RL - 6, 0, 8)
    block(3, RL - 6, CL - 8, 8)

    def strips(j, carry):
        col0 = pl.multiple_of(j * STRIP, 8)
        block(0, 3, col0, STRIP)
        block(RL - 3, 3, col0, STRIP)
        return carry

    lax.fori_loop(0, CL // STRIP, strips, 0, unroll=STRIP_UNROLL)

    attended = att[...].reshape(RL * CL, C).astype(BF16)
    d_query = (dq[...] * 0.125).reshape(RL * CL, C).astype(BF16)
    cot_rows = cot[...].reshape(RL * CL, C)
    u = u_ext[...].reshape(RE * CE, C).astype(BF16)
    d_kv = jnp.concatenate(
        [dk_ext[...].reshape(RE * CE, C).astype(BF16), dv_ext[...].reshape(RE * CE, C).astype(BF16)], axis=-1
    )
    g_kv = dot(u, d_kv, TN)
    gsum[0:C, :] = dot(unit.astype(BF16), d_query, TN)
    gsum[C : 2 * C, :] = g_kv[:, 0:C]
    gsum[2 * C : 3 * C, :] = g_kv[:, C : 2 * C]
    gsum[3 * C : 4 * C, :] = dot(attended, cot_rows, TN)
    g16[...] = gsum[...].astype(BF16)
    for d in range(1, na):
        m, device = plane(d)
        pltpu.make_async_remote_copy(
            g16.at[pl.ds(pl.multiple_of(m * rows, rows), rows)],
            rs_rx.at[pl.ds((d - 1) * rows, rows)],
            a_send.at[0], a_recv.at[0], device_id=device, device_id_type=MESH,
        ).start()

    dn_ext[...] = dot(d_kv, wqkv[:, C : 3 * C], NT).reshape(RE, CE, C)
    pad_rows = jnp.zeros((8, C), F32)
    for i, lo in enumerate((0, RL + 3)):
        flat = dn_ext[lo : lo + 3].reshape(3 * CE, C)
        tx2_rows[i] = jnp.concatenate([flat, pad_rows], axis=0).astype(BF16)
        for k, left in enumerate((0, CL)):
            corner = dn_ext[lo : lo + 3, left : left + 8].reshape(24, C)
            tx2_corner[2 * i + k] = jnp.concatenate([corner, pad_rows], axis=0).astype(BF16)
    for k, left in enumerate((0, CL)):
        tx2_cols[k] = dn_ext[3 : RL + 3, left : left + 8].reshape(RL * 8, C).astype(BF16)
    back = []
    for i, (dr, dc) in enumerate(around):
        if dc == 0:
            n = 0 if dr < 0 else 1
            src, dst = tx2_rows.at[n], rx2_rows.at[n]
        elif dr == 0:
            n = 0 if dc < 0 else 1
            src, dst = tx2_cols.at[n], rx2_cols.at[n]
        else:
            n = (0 if dr < 0 else 2) + (0 if dc < 0 else 1)
            src, dst = tx2_corner.at[n], rx2_corner.at[n]
        copy = pltpu.make_async_remote_copy(
            src, dst, d_send.at[i], d_recv.at[i], device_id=beside(dr, dc), device_id_type=MESH
        )
        copy.start()
        back.append(copy)

    x = tok[...].astype(F32).reshape(RL * CL, C)
    out[...] = (x + dot(attended, wout[...])).astype(BF16).reshape(RL, CL, C)
    writes = [
        pltpu.make_async_copy(src, dst, out_sem.at[i])
        for i, (src, dst) in enumerate(
            ((out, out_hbm), (tgrad, tgrad_hbm), (qkvg, qkvg_hbm), (outg, outg_hbm), (gaing, gaing_hbm))
        )
    ]
    writes[0].start()
    for copy, _, to, _ in halo:
        pl.when(to)(copy.wait_send)

    wait_bytes(rs_rx, a_recv.at[0])
    mine = gsum[pl.ds(pl.multiple_of(me * rows, rows), rows), :]
    parts = rs_rx[...].astype(F32).reshape(na - 1, rows, C)
    z_rx[pl.ds(z, 1)] = (mine + jnp.sum(parts, axis=0)).astype(BF16)[None]
    for d in range(1, zn):
        pltpu.make_async_remote_copy(
            z_rx.at[z], z_rx.at[z],
            a_send.at[1], a_recv.at[1], device_id=column(d), device_id_type=MESH,
        ).start()

    for copy in back:
        copy.wait()
    sub = lax.broadcasted_iota(jnp.int32, (1, 8, 1), 1)
    tile = lax.broadcasted_iota(jnp.int32, (1, CE, 1), 1)
    middle = (tile >= 4) & (tile < CL + 4)

    def add(rsl, csl, rx, n, mask):
        shape = (rsl.stop - rsl.start, csl.stop - csl.start, C)
        more = rx[n].astype(F32)[0 : shape[0] * shape[1]].reshape(shape)
        dn_ext[rsl, csl, :] += jnp.where(mask, more, 0.0)

    first, last = slice(3, 6), slice(RL, RL + 3)
    left, right = slice(0, 8), slice(CL, CE)
    add(last, slice(0, CE), rx2_rows, 0, middle)
    add(first, slice(0, CE), rx2_rows, 1, middle)
    add(slice(3, RL + 3), right, rx2_cols, 0, sub < 4)
    add(slice(3, RL + 3), left, rx2_cols, 1, sub >= 4)
    add(last, right, rx2_corner, 0, sub < 4)
    add(last, left, rx2_corner, 1, sub >= 4)
    add(first, right, rx2_corner, 2, sub < 4)
    add(first, left, rx2_corner, 3, sub >= 4)
    d_normed = dot(d_query, wqkv[:, 0:C], NT) + dn_ext[3 : RL + 3, 4 : CL + 4, :].reshape(RL * CL, C)
    x = tok[...].astype(F32).reshape(RL * CL, C)
    r = inverse_rms(x)
    unit = x * r
    g = d_normed * gains
    mean = jnp.sum(g * unit, axis=-1, keepdims=True) * (1.0 / C)
    grads = cot_rows.astype(F32) + r * (g - unit * mean)
    tgrad[...] = grads.astype(BF16).reshape(RL, CL, C)
    writes[1].start()

    wait_bytes(z_rx.at[pl.ds(0, zn - 1)], a_recv.at[1])
    here = pl.ds(pl.multiple_of(me * rows, rows), rows)
    ag[here, :] = jnp.sum(z_rx[...].astype(F32), axis=0).astype(BF16)
    for d in range(1, na):
        m, device = plane(d)
        pltpu.make_async_remote_copy(
            ag.at[here], ag.at[here],
            a_send.at[2], a_recv.at[2], device_id=device, device_id_type=MESH,
        ).start()
    eye = lax.broadcasted_iota(jnp.int32, (C, C), 0) == lax.broadcasted_iota(jnp.int32, (C, C), 1)
    gain_col = jnp.sum(jnp.where(eye, gains, 0.0), axis=1, keepdims=True)
    wait_bytes(z_rx.at[pl.ds(0, zn - 1)], a_send.at[1])
    wait_bytes(rs_rx, a_send.at[0])
    wait_bytes(rs_rx, a_recv.at[2])
    factor = (gxn * RL * gyn * CL) ** (-0.5)
    total = jnp.zeros((C, C), F32)
    for i in range(3):
        piece = ag[i * C : (i + 1) * C, :].astype(F32) * factor
        qkvg[:, i * C : (i + 1) * C] = piece * gain_col
        total += piece * wqkv[:, i * C : (i + 1) * C].astype(F32)
    writes[2].start()
    outg[...] = ag[3 * C : 4 * C, :].astype(F32) * factor
    writes[3].start()
    gain_sum = jnp.sum(total, axis=1, keepdims=True)
    gaing[...] = jnp.sum(jnp.where(eye, gain_sum, 0.0), axis=0, keepdims=True)
    writes[4].start()
    wait_bytes(rs_rx, a_send.at[2])
    for write in writes:
        write.wait()


def finish(*refs):
    held, sem = refs[10:15], refs[15]
    reads = [pltpu.make_async_copy(refs[i], held[i], sem.at[0, i]) for i in range(5)]
    writes = [pltpu.make_async_copy(held[i], refs[5 + i], sem.at[1, i]) for i in range(5)]
    for read in reads:
        read.start()
    for read, write in zip(reads, writes):
        read.wait()
        write.start()
    for write in writes:
        write.wait()


def per_device(gxn, gyn, zn, tokens, norm_gain, qkv_weight, output_weight, cotangent):
    na = (gxn // zn) * gyn
    rows = 512 // na
    hbm = pl.BlockSpec(memory_space=pl.ANY)
    results = (
        jax.ShapeDtypeStruct((RL, CL, C), BF16),
        jax.ShapeDtypeStruct((RL, CL, C), BF16),
        jax.ShapeDtypeStruct((C, 3 * C), F32),
        jax.ShapeDtypeStruct((C, C), F32),
        jax.ShapeDtypeStruct((1, C), F32),
    )
    image = pltpu.VMEM((RL, CL, C), BF16)
    image32 = pltpu.VMEM((RL, CL, C), F32)
    ext32 = pltpu.VMEM((RE, CE, C), F32)
    dma = pltpu.SemaphoreType.DMA
    raw = pl.pallas_call(
        functools.partial(kernel, gxn, gyn, zn),
        out_shape=results,
        in_specs=[hbm] * 5,
        out_specs=(hbm,) * 5,
        scratch_shapes=[
            image,
            pltpu.VMEM((1, C), F32),
            pltpu.VMEM((C, 3 * C), BF16),
            pltpu.VMEM((C, C), BF16),
            image,
            image,
            image,
            pltpu.VMEM((C, 3 * C), F32),
            pltpu.VMEM((C, C), F32),
            pltpu.VMEM((1, C), F32),
            pltpu.VMEM((2, 3, CL, C), BF16),
            pltpu.VMEM((2, RL, 16, C), BF16),
            pltpu.VMEM((4, 3, 16, C), BF16),
            ext32, ext32, ext32, ext32, ext32, ext32,
            image32, image32, image32, image32,
            pltpu.VMEM((2, 224, C), BF16),
            pltpu.VMEM((2, RL * 8, C), BF16),
            pltpu.VMEM((4, 32, C), BF16),
            pltpu.VMEM((2, 224, C), BF16),
            pltpu.VMEM((2, RL * 8, C), BF16),
            pltpu.VMEM((4, 32, C), BF16),
            pltpu.VMEM((4 * C, C), F32),
            pltpu.VMEM((4 * C, C), BF16),
            pltpu.VMEM(((na - 1) * rows, C), BF16),
            pltpu.VMEM((zn, rows, C), BF16),
            pltpu.VMEM((4 * C, C), BF16),
            dma((5,)), dma((5,)), dma((8,)), dma((8,)), dma((8,)), dma((8,)), dma((3,)), dma((3,)),
        ],
        compiler_params=pltpu.CompilerParams(
            collective_id=0, has_side_effects=True, vmem_limit_bytes=60 << 20
        ),
    )(
        tokens.reshape(RL, CL, C),
        norm_gain.reshape(1, C),
        qkv_weight,
        output_weight,
        cotangent.reshape(RL, CL, C),
    )
    out, tgrad, qkvg, outg, gaing = pl.pallas_call(
        finish,
        out_shape=results,
        in_specs=[hbm] * 5,
        out_specs=(hbm,) * 5,
        scratch_shapes=[pltpu.VMEM(r.shape, r.dtype) for r in results] + [dma((2, 5))],
        compiler_params=pltpu.CompilerParams(vmem_limit_bytes=60 << 20),
    )(*raw)
    return (
        out.reshape(tokens.shape),
        tgrad.reshape(tokens.shape),
        qkvg,
        outg,
        gaing.reshape(C),
    )


def solution(mesh):
    gxn, gyn = mesh.shape["gx"], mesh.shape["gy"]
    image = P(None, "gx", "gy", None)
    return jax.shard_map(
        functools.partial(per_device, gxn, gyn, min(ZN, max(gxn // 4, 2))),
        mesh=mesh,
        in_specs=(image, P(), P(), P(), image),
        out_specs=(image, image, P(), P(), P()),
        check_vma=False,
    )
```

```python
import functools

import jax
import jax.numpy as jnp
from jax import lax
from jax.experimental import pallas as pl
from jax.experimental.pallas import tpu as pltpu
from jax.sharding import PartitionSpec as P

MESH = pl.DeviceIdType.MESH
EPS = 1e-06
F32 = jnp.float32
BF16 = jnp.bfloat16
C = 128
RL, CL = 16, 64
RE, CE = RL + 6, CL + 8
NB = CL // 8
STRIP = 32
NEG = -1e30
ZN = 8

NT = (((1,), (1,)), ((), ()))
TN = (((0,), (0,)), ((), ()))


def dot(a, b, dims=(((1,), (0,)), ((), ()))):
    return lax.dot_general(a, b, dims, preferred_element_type=F32)


def inverse_rms(x):
    return lax.rsqrt(jnp.sum(x * x, axis=-1, keepdims=True) * (1.0 / C) + EPS)


def kernel(
    gxn, gyn, zn,
    tok_hbm, gain_hbm, wqkv_hbm, wout_hbm, cot_hbm,
    out_hbm, tgrad_hbm, summed_hbm,
    tok, gain, wqkv, wout, cot,
    out, tgrad,
    rx_rows, rx_cols, rx_corner,
    u_ext, k_ext, v_ext, dk_ext, dv_ext, dn_ext,
    q_loc, da_loc, att, dq,
    tx2_rows, tx2_cols, tx2_corner, rx2_rows, rx2_cols, rx2_corner,
    gsum, g16, rs_rx, z_rx, own,
    in_sem, out_sem, h_send, h_recv, d_send, d_recv, a_send, a_recv,
):
    yn = gxn // zn
    na = yn * gyn
    rows = 512 // na
    gx = lax.axis_index("gx")
    gy = lax.axis_index("gy")
    y, z = lax.div(gx, zn), lax.rem(gx, zn)
    me = y * gyn + gy
    ys = [lax.rem(y + d, yn) * zn + z for d in range(yn)]
    cs = [lax.rem(gy + d, gyn) for d in range(gyn)]
    zs = [y * zn + lax.rem(z + d, zn) for d in range(zn)]

    def far(d, n):
        return min(d, n - d)

    plane = sorted(
        ((dy, dc) for dy in range(yn) for dc in range(gyn) if dy or dc),
        key=lambda o: (-far(o[0], yn) - far(o[1], gyn) / 2, o),
    )
    column = sorted(range(1, zn), key=lambda d: (-far(d, zn), d))

    def beside(dr, dc):
        return (lax.rem(gx + (dr + gxn), gxn) if dr else gx, cs[dc % gyn])

    def exists(dr, dc):
        r, c = gx + dr, gy + dc
        return (r >= 0) & (r < gxn) & (c >= 0) & (c < gyn)

    def wait_bytes(ref, sem):
        pltpu.make_async_copy(ref, ref, sem).wait()

    fetches = [
        pltpu.make_async_copy(src, dst, in_sem.at[i])
        for i, (src, dst) in enumerate(
            ((tok_hbm, tok), (gain_hbm, gain), (wqkv_hbm, wqkv), (cot_hbm, cot), (wout_hbm, wout))
        )
    ]
    around = [(dr, dc) for dr in (-1, 0, 1) for dc in (-1, 0, 1) if dr or dc]
    barrier = pltpu.get_barrier_semaphore()

    def greet(device):
        pl.semaphore_signal(barrier, inc=1, device_id=device, device_id_type=MESH)

    for fetch in fetches:
        fetch.start()
    for dr, dc in around:
        if dr:
            greet(beside(dr, dc))
    for dy, dc in reversed(plane):
        greet((ys[dy], cs[dc]))
    for d in reversed(column):
        greet((zs[d], gy))
    fetches[0].wait()
    pl.semaphore_wait(barrier, 6 + (zn - 1) + (na - 1))

    halo = []
    for i, (dr, dc) in enumerate(around):
        rsl = slice(0, RL) if dr == 0 else (slice(0, 3) if dr < 0 else slice(RL - 3, RL))
        csl = slice(0, CL) if dc == 0 else (slice(0, 16) if dc < 0 else slice(CL - 16, CL))
        src = tok.at[rsl, csl]
        if dc == 0:
            dst = rx_rows.at[0 if dr > 0 else 1]
        elif dr == 0:
            dst = rx_cols.at[0 if dc > 0 else 1]
        else:
            dst = rx_corner.at[(0 if dr > 0 else 2) + (0 if dc > 0 else 1)]
        copy = pltpu.make_async_remote_copy(
            src, dst, h_send.at[i], h_recv.at[i], device_id=beside(dr, dc), device_id_type=MESH
        )
        halo.append((copy, dst, exists(dr, dc), exists(-dr, -dc)))
    for copy, dst, to, _ in halo:
        pl.when(to)(copy.start)

    for fetch in fetches[1:]:
        fetch.wait()
    dk_ext[...] = jnp.zeros_like(dk_ext)
    dv_ext[...] = jnp.zeros_like(dv_ext)
    u_ext[...] = jnp.zeros_like(u_ext)
    gains = gain[...]

    def keyval(unit):
        return dot((unit * gains).astype(BF16), wqkv[:, C : 3 * C])

    x = tok[...].astype(F32).reshape(RL * CL, C)
    unit = x * inverse_rms(x)
    normed = (unit * gains).astype(BF16)
    u_ext[3 : RL + 3, 4 : CL + 4, :] = unit.reshape(RL, CL, C)
    projected = dot(normed, wqkv[...])
    q_loc[...] = (projected[:, 0:C] * 0.125).reshape(RL, CL, C)
    k_ext[3 : RL + 3, 4 : CL + 4, :] = projected[:, C : 2 * C].reshape(RL, CL, C)
    v_ext[3 : RL + 3, 4 : CL + 4, :] = projected[:, 2 * C : 3 * C].reshape(RL, CL, C)
    da_loc[...] = dot(cot[...].reshape(RL * CL, C), wout[...], NT).reshape(RL, CL, C)

    head0 = lax.broadcasted_iota(jnp.int32, (1, C), 1) < 64

    def two_heads(v):
        v = v.astype(BF16)
        zero = jnp.zeros_like(v)
        return jnp.concatenate([jnp.where(head0, v, zero), jnp.where(head0, zero, v)], axis=0)

    def block(row0, nr, col0, nc):
        kr, kc, nq = nr + 6, nc + 8, nr * nc
        lanes = 2 * nq
        keys = (slice(row0, row0 + kr), pl.ds(col0, kc))
        own = (slice(row0, row0 + nr), pl.ds(col0, nc))
        at = lax.broadcasted_iota(jnp.int32, (1, 1, lanes), 2) % nq
        q_row, q_col = at // nc, at % nc
        key_row = lax.broadcasted_iota(jnp.int32, (kr, 1, lanes), 0)
        key_col = lax.broadcasted_iota(jnp.int32, (1, kc, lanes), 1)
        image_row = gx * RL + row0 - 3 + key_row
        image_col = gy * CL + col0 - 4 + key_col
        row_bias = jnp.where(
            (key_row >= q_row) & (key_row <= q_row + 6) & (image_row >= 0) & (image_row < gxn * RL), 0.0, NEG
        )
        col_bias = jnp.where(
            (key_col >= q_col + 1) & (key_col <= q_col + 7) & (image_col >= 0) & (image_col < gyn * CL), 0.0, NEG
        )
        kw = k_ext[keys[0], keys[1], :].reshape(kr * kc, C).astype(BF16)
        vw = v_ext[keys[0], keys[1], :].reshape(kr * kc, C).astype(BF16)
        qb = two_heads(q_loc[own[0], own[1], :].reshape(nq, C))
        db = two_heads(da_loc[own[0], own[1], :].reshape(nq, C))
        scores = dot(kw, qb, NT).reshape(kr, kc, lanes)
        weights = jnp.exp(scores + row_bias + col_bias).reshape(kr * kc, lanes)
        totals = jnp.sum(weights, axis=0, keepdims=True)
        shares = weights * (1.0 / totals)
        shares_low = shares.astype(BF16)
        d_shares = dot(vw, db, NT)
        delta = jnp.sum(shares * d_shares, axis=0, keepdims=True)
        d_scores = (shares * (d_shares - delta)).astype(BF16)
        a2 = dot(shares_low, vw, TN)
        dq2 = dot(d_scores, kw, TN)
        att[own[0], own[1], :] = jnp.where(head0, a2[0:nq], a2[nq:]).reshape(nr, nc, C)
        dq[own[0], own[1], :] = jnp.where(head0, dq2[0:nq], dq2[nq:]).reshape(nr, nc, C)
        dk_ext[keys[0], keys[1], :] += dot(d_scores, qb).reshape(kr, kc, C)
        dv_ext[keys[0], keys[1], :] += dot(shares_low, db).reshape(kr, kc, C)

    for j in range(1, NB - 1):
        block(3, RL - 6, j * 8, 8)

    for copy, dst, _, come in halo:
        pl.when(come)(copy.wait_recv)

        @pl.when(jnp.logical_not(come))
        def _():
            dst[...] = jnp.zeros(dst.shape, BF16)

    rims = (
        (rx_rows[0].astype(F32), slice(0, 3), slice(4, CL + 4), slice(0, CL)),
        (rx_rows[1].astype(F32), slice(RL + 3, RE), slice(4, CL + 4), slice(0, CL)),
        (rx_cols[0].astype(F32)[:, 8:16], slice(3, RL + 3), slice(0, 4), slice(4, 8)),
        (rx_cols[1].astype(F32)[:, 0:8], slice(3, RL + 3), slice(CL + 4, CE), slice(0, 4)),
        (rx_corner[0].astype(F32)[:, 8:16], slice(0, 3), slice(0, 4), slice(4, 8)),
        (rx_corner[1].astype(F32)[:, 0:8], slice(0, 3), slice(CL + 4, CE), slice(0, 4)),
        (rx_corner[2].astype(F32)[:, 8:16], slice(RL + 3, RE), slice(0, 4), slice(4, 8)),
        (rx_corner[3].astype(F32)[:, 0:8], slice(RL + 3, RE), slice(CL + 4, CE), slice(0, 4)),
    )
    xh = jnp.concatenate([rim[0].reshape(-1, C) for rim in rims], axis=0)
    uh = xh * inverse_rms(xh)
    kvh = keyval(uh)
    start = 0
    for tokens, rsl, csl, used in rims:
        shape = tokens.shape
        n = shape[0] * shape[1]
        u_ext[rsl, csl, :] = uh[start : start + n].reshape(shape)[:, used]
        k_ext[rsl, csl, :] = kvh[start : start + n, 0:C].reshape(shape)[:, used]
        v_ext[rsl, csl, :] = kvh[start : start + n, C : 2 * C].reshape(shape)[:, used]
        start += n

    block(3, RL - 6, 0, 8)
    block(3, RL - 6, CL - 8, 8)

    for col0 in range(0, CL, STRIP):
        block(0, 3, col0, STRIP)
        block(RL - 3, 3, col0, STRIP)

    attended = att[...].reshape(RL * CL, C).astype(BF16)
    d_query = (dq[...] * 0.125).reshape(RL * CL, C).astype(BF16)
    cot_rows = cot[...].reshape(RL * CL, C)
    u = u_ext[...].reshape(RE * CE, C).astype(BF16)
    d_kv = jnp.concatenate(
        [dk_ext[...].reshape(RE * CE, C).astype(BF16), dv_ext[...].reshape(RE * CE, C).astype(BF16)], axis=-1
    )
    g_kv = dot(u, d_kv, TN)
    gsum[0:C, :] = dot(unit.astype(BF16), d_query, TN)
    gsum[C : 2 * C, :] = g_kv[:, 0:C]
    gsum[2 * C : 3 * C, :] = g_kv[:, C : 2 * C]
    gsum[3 * C : 4 * C, :] = dot(attended, cot_rows, TN)
    g16[...] = gsum[...].astype(BF16)
    bases = [lax.rem(y + d, yn) * gyn for d in range(yn)]
    for i, (dy, dc) in enumerate(plane):
        m = bases[dy] + cs[dc]
        pltpu.make_async_remote_copy(
            g16.at[pl.ds(pl.multiple_of(m * rows, rows), rows)],
            rs_rx.at[pl.ds(i * rows, rows)],
            a_send.at[0], a_recv.at[0], device_id=(ys[dy], cs[dc]), device_id_type=MESH,
        ).start()

    dn_ext[...] = dot(d_kv, wqkv[:, C : 3 * C], NT).reshape(RE, CE, C)
    pad_rows = jnp.zeros((8, C), F32)
    for i, lo in enumerate((0, RL + 3)):
        flat = dn_ext[lo : lo + 3].reshape(3 * CE, C)
        tx2_rows[i] = jnp.concatenate([flat, pad_rows], axis=0).astype(BF16)
        for k, left in enumerate((0, CL)):
            corner = dn_ext[lo : lo + 3, left : left + 8].reshape(24, C)
            tx2_corner[2 * i + k] = jnp.concatenate([corner, pad_rows], axis=0).astype(BF16)
    for k, left in enumerate((0, CL)):
        tx2_cols[k] = dn_ext[3 : RL + 3, left : left + 8].reshape(RL * 8, C).astype(BF16)
    back = []
    for i, (dr, dc) in enumerate(around):
        if dc == 0:
            n = 0 if dr < 0 else 1
            src, dst = tx2_rows.at[n], rx2_rows.at[n]
        elif dr == 0:
            n = 0 if dc < 0 else 1
            src, dst = tx2_cols.at[n], rx2_cols.at[n]
        else:
            n = (0 if dr < 0 else 2) + (0 if dc < 0 else 1)
            src, dst = tx2_corner.at[n], rx2_corner.at[n]
        copy = pltpu.make_async_remote_copy(
            src, dst, d_send.at[i], d_recv.at[i], device_id=beside(dr, dc), device_id_type=MESH
        )
        copy.start()
        back.append(copy)

    x = tok[...].astype(F32).reshape(RL * CL, C)
    out[...] = (x + dot(attended, wout[...])).astype(BF16).reshape(RL, CL, C)
    here = pl.ds(pl.multiple_of(me * rows, rows), rows)
    writes = [
        pltpu.make_async_copy(src, dst, out_sem.at[i])
        for i, (src, dst) in enumerate(
            ((out, out_hbm), (tgrad, tgrad_hbm), (own, summed_hbm.at[here]))
        )
    ]
    writes[0].start()
    for copy, _, to, _ in halo:
        pl.when(to)(copy.wait_send)

    wait_bytes(rs_rx, a_recv.at[0])
    mine = gsum[pl.ds(pl.multiple_of(me * rows, rows), rows), :]
    parts = rs_rx[...].astype(F32).reshape(na - 1, rows, C)
    z_rx[pl.ds(z, 1)] = (mine + jnp.sum(parts, axis=0)).astype(BF16)[None]
    for d in column:
        pltpu.make_async_remote_copy(
            z_rx.at[z], z_rx.at[z],
            a_send.at[1], a_recv.at[1], device_id=(zs[d], gy), device_id_type=MESH,
        ).start()

    for copy in back:
        copy.wait()
    sub = lax.broadcasted_iota(jnp.int32, (1, 8, 1), 1)
    tile = lax.broadcasted_iota(jnp.int32, (1, CE, 1), 1)
    middle = (tile >= 4) & (tile < CL + 4)

    def add(rsl, csl, rx, n, mask):
        shape = (rsl.stop - rsl.start, csl.stop - csl.start, C)
        more = rx[n].astype(F32)[0 : shape[0] * shape[1]].reshape(shape)
        dn_ext[rsl, csl, :] += jnp.where(mask, more, 0.0)

    first, last = slice(3, 6), slice(RL, RL + 3)
    left, right = slice(0, 8), slice(CL, CE)
    add(last, slice(0, CE), rx2_rows, 0, middle)
    add(first, slice(0, CE), rx2_rows, 1, middle)
    add(slice(3, RL + 3), right, rx2_cols, 0, sub < 4)
    add(slice(3, RL + 3), left, rx2_cols, 1, sub >= 4)
    add(last, right, rx2_corner, 0, sub < 4)
    add(last, left, rx2_corner, 1, sub >= 4)
    add(first, right, rx2_corner, 2, sub < 4)
    add(first, left, rx2_corner, 3, sub >= 4)
    d_normed = dot(d_query, wqkv[:, 0:C], NT) + dn_ext[3 : RL + 3, 4 : CL + 4, :].reshape(RL * CL, C)
    x = tok[...].astype(F32).reshape(RL * CL, C)
    r = inverse_rms(x)
    unit = x * r
    g = d_normed * gains
    mean = jnp.sum(g * unit, axis=-1, keepdims=True) * (1.0 / C)
    grads = cot_rows.astype(F32) + r * (g - unit * mean)
    tgrad[...] = grads.astype(BF16).reshape(RL, CL, C)
    writes[1].start()

    wait_bytes(z_rx.at[pl.ds(0, zn - 1)], a_recv.at[1])
    own[...] = jnp.sum(z_rx[...].astype(F32), axis=0).astype(BF16)
    for dy, dc in plane:
        pltpu.make_async_remote_copy(
            own, summed_hbm.at[here],
            a_send.at[2], a_recv.at[2], device_id=(ys[dy], cs[dc]), device_id_type=MESH,
        ).start()
    writes[2].start()
    wait_bytes(z_rx.at[pl.ds(0, zn - 1)], a_send.at[1])
    wait_bytes(rs_rx, a_send.at[0])
    for write in writes:
        write.wait()
    wait_bytes(rs_rx, a_recv.at[2])
    wait_bytes(rs_rx, a_send.at[2])


def finish(
    factor, out, tgrad, summed, gain, wqkv, out_hbm, tgrad_hbm, qkvg_hbm, outg_hbm, gaing_hbm,
    out_v, tgrad_v, summed_v, gain_v, wqkv_v, qkvg, outg, gaing, r_sem, w_sem,
):
    held = ((summed, summed_v), (gain, gain_v), (wqkv, wqkv_v), (out, out_v), (tgrad, tgrad_v))
    reads = [pltpu.make_async_copy(src, dst, r_sem.at[i]) for i, (src, dst) in enumerate(held)]
    made = ((qkvg, qkvg_hbm), (outg, outg_hbm), (gaing, gaing_hbm), (out_v, out_hbm), (tgrad_v, tgrad_hbm))
    writes = [pltpu.make_async_copy(src, dst, w_sem.at[i]) for i, (src, dst) in enumerate(made)]
    for read in reads:
        read.start()
    eye = lax.broadcasted_iota(jnp.int32, (C, C), 0) == lax.broadcasted_iota(jnp.int32, (C, C), 1)
    for read in reads:
        read.wait()
    writes[3].start()
    writes[4].start()
    gain_col = jnp.sum(jnp.where(eye, gain_v[...], 0.0), axis=1, keepdims=True)
    total = jnp.zeros((C, C), F32)
    for i in range(3):
        piece = summed_v[i * C : (i + 1) * C, :].astype(F32) * factor
        qkvg[:, i * C : (i + 1) * C] = piece * gain_col
        total += piece * wqkv_v[:, i * C : (i + 1) * C].astype(F32)
    writes[0].start()
    outg[...] = summed_v[3 * C : 4 * C, :].astype(F32) * factor
    writes[1].start()
    gain_sum = jnp.sum(total, axis=1, keepdims=True)
    gaing[...] = jnp.sum(jnp.where(eye, gain_sum, 0.0), axis=0, keepdims=True)
    writes[2].start()
    for write in writes:
        write.wait()


def per_device(gxn, gyn, zn, tokens, norm_gain, qkv_weight, output_weight, cotangent):
    na = (gxn // zn) * gyn
    rows = 512 // na
    gain_row = norm_gain.reshape(1, C)
    hbm = pl.BlockSpec(memory_space=pl.ANY)
    images = (jax.ShapeDtypeStruct((RL, CL, C), BF16),) * 2
    results = images + (
        jax.ShapeDtypeStruct((C, 3 * C), F32),
        jax.ShapeDtypeStruct((C, C), F32),
        jax.ShapeDtypeStruct((1, C), F32),
    )
    image = pltpu.VMEM((RL, CL, C), BF16)
    image32 = pltpu.VMEM((RL, CL, C), F32)
    ext32 = pltpu.VMEM((RE, CE, C), F32)
    dma = pltpu.SemaphoreType.DMA
    raw = pl.pallas_call(
        functools.partial(kernel, gxn, gyn, zn),
        out_shape=images + (jax.ShapeDtypeStruct((4 * C, C), BF16),),
        in_specs=[hbm] * 5,
        out_specs=(hbm,) * 3,
        scratch_shapes=[
            image,
            pltpu.VMEM((1, C), F32),
            pltpu.VMEM((C, 3 * C), BF16),
            pltpu.VMEM((C, C), BF16),
            image,
            image,
            image,
            pltpu.VMEM((2, 3, CL, C), BF16),
            pltpu.VMEM((2, RL, 16, C), BF16),
            pltpu.VMEM((4, 3, 16, C), BF16),
            ext32, ext32, ext32, ext32, ext32, ext32,
            image32, image32, image32, image32,
            pltpu.VMEM((2, 224, C), BF16),
            pltpu.VMEM((2, RL * 8, C), BF16),
            pltpu.VMEM((4, 32, C), BF16),
            pltpu.VMEM((2, 224, C), BF16),
            pltpu.VMEM((2, RL * 8, C), BF16),
            pltpu.VMEM((4, 32, C), BF16),
            pltpu.VMEM((4 * C, C), F32),
            pltpu.VMEM((4 * C, C), BF16),
            pltpu.VMEM(((na - 1) * rows, C), BF16),
            pltpu.VMEM((zn, rows, C), BF16),
            pltpu.VMEM((rows, C), BF16),
            dma((5,)), dma((3,)), dma((8,)), dma((8,)), dma((8,)), dma((8,)), dma((3,)), dma((3,)),
        ],
        compiler_params=pltpu.CompilerParams(
            collective_id=0, has_side_effects=True, vmem_limit_bytes=60 << 20
        ),
    )(
        tokens.reshape(RL, CL, C),
        gain_row,
        qkv_weight,
        output_weight,
        cotangent.reshape(RL, CL, C),
    )
    out, tgrad, qkvg, outg, gaing = pl.pallas_call(
        functools.partial(finish, (gxn * RL * gyn * CL) ** (-0.5)),
        out_shape=results,
        in_specs=[hbm] * 5,
        out_specs=(hbm,) * 5,
        scratch_shapes=[
            image,
            image,
            pltpu.VMEM((4 * C, C), BF16),
            pltpu.VMEM((1, C), F32),
            pltpu.VMEM((C, 3 * C), BF16),
            pltpu.VMEM((C, 3 * C), F32),
            pltpu.VMEM((C, C), F32),
            pltpu.VMEM((1, C), F32),
            dma((5,)),
            dma((5,)),
        ],
        compiler_params=pltpu.CompilerParams(vmem_limit_bytes=60 << 20),
    )(*raw, gain_row, qkv_weight)
    return (
        out.reshape(tokens.shape),
        tgrad.reshape(tokens.shape),
        qkvg,
        outg,
        gaing.reshape(C),
    )


def solution(mesh):
    gxn, gyn = mesh.shape["gx"], mesh.shape["gy"]
    image = P(None, "gx", "gy", None)
    return jax.shard_map(
        functools.partial(per_device, gxn, gyn, min(ZN, max(gxn // 4, 2))),
        mesh=mesh,
        in_specs=(image, P(), P(), P(), image),
        out_specs=(image, image, P(), P(), P()),
        check_vma=False,
    )
```

```python
import functools

import jax
import jax.numpy as jnp
from jax import lax
from jax.experimental import pallas as pl
from jax.experimental.pallas import tpu as pltpu
from jax.sharding import PartitionSpec as P

MESH = pl.DeviceIdType.MESH
EPS = 1e-06
F32 = jnp.float32
BF16 = jnp.bfloat16
C = 128
RL, CL = 16, 64
RE, CE = RL + 6, CL + 8
NB = CL // 8
STRIP = 16
NEG = -1e30
ZN = 8

NT = (((1,), (1,)), ((), ()))
TN = (((0,), (0,)), ((), ()))


def dot(a, b, dims=(((1,), (0,)), ((), ()))):
    return lax.dot_general(a, b, dims, preferred_element_type=F32)


def inverse_rms(x):
    return lax.rsqrt(jnp.sum(x * x, axis=-1, keepdims=True) * (1.0 / C) + EPS)


def kernel(
    gxn, gyn, zn,
    tok_hbm, gain_hbm, wqkv_hbm, wout_hbm, cot_hbm,
    out_hbm, tgrad_hbm, summed_hbm,
    tok, gain, wqkv, wout, cot,
    out, tgrad,
    tx_cols, tx_corner, rx_rows, rx_cols, rx_corner,
    u_ext, k_ext, v_ext, dk_ext, dv_ext, dn_ext,
    q_loc, da_loc, att, dq,
    tx2_rows, tx2_cols, tx2_corner, rx2_rows, rx2_cols, rx2_corner,
    gsum, g16, rs_rx, z_rx, own,
    in_sem, out_sem, h_send, h_recv, d_send, d_recv, a_send, a_recv,
):
    yn = gxn // zn
    na = yn * gyn
    rows = 512 // na
    gx = lax.axis_index("gx")
    gy = lax.axis_index("gy")
    y, z = lax.div(gx, zn), lax.rem(gx, zn)
    me = y * gyn + gy
    ys = [lax.rem(y + d, yn) * zn + z for d in range(yn)]
    cs = [lax.rem(gy + d, gyn) for d in range(gyn)]
    zs = [y * zn + lax.rem(z + d, zn) for d in range(zn)]

    def far(d, n):
        return min(d, n - d)

    plane = sorted(
        ((dy, dc) for dy in range(yn) for dc in range(gyn) if dy or dc),
        key=lambda o: (-far(o[0], yn) - far(o[1], gyn) / 2, o),
    )
    column = sorted(range(1, zn), key=lambda d: (-far(d, zn), d))

    def beside(dr, dc):
        return (lax.rem(gx + (dr + gxn), gxn) if dr else gx, cs[dc % gyn])

    def exists(dr, dc):
        r, c = gx + dr, gy + dc
        return (r >= 0) & (r < gxn) & (c >= 0) & (c < gyn)

    def wait_bytes(ref, sem):
        pltpu.make_async_copy(ref, ref, sem).wait()

    fetches = [
        pltpu.make_async_copy(src, dst, in_sem.at[i])
        for i, (src, dst) in enumerate(
            ((tok_hbm, tok), (gain_hbm, gain), (wqkv_hbm, wqkv), (cot_hbm, cot), (wout_hbm, wout))
        )
    ]
    around = [(-1, 0), (1, 0), (-1, -1), (-1, 1), (1, -1), (1, 1), (0, -1), (0, 1)]
    barrier = pltpu.get_barrier_semaphore()

    def greet(device):
        pl.semaphore_signal(barrier, inc=1, device_id=device, device_id_type=MESH)

    for fetch in fetches:
        fetch.start()
    for dr, dc in around:
        if dr:
            greet(beside(dr, dc))
    for dy, dc in reversed(plane):
        greet((ys[dy], cs[dc]))
    for d in reversed(column):
        greet((zs[d], gy))
    fetches[0].wait()
    pl.semaphore_wait(barrier, 6 + (zn - 1) + (na - 1))

    def packed(v):
        if v.shape[0] == 3:
            v = jnp.concatenate([v, v[0:1]], axis=0)
        half = v.shape[0] // 2
        return jnp.concatenate([v[0:half], v[half:]], axis=1).reshape(half * 8, C).astype(BF16)

    def unpacked(v):
        v = v.reshape(-1, 8, C)
        return jnp.concatenate([v[:, 0:4], v[:, 4:8]], axis=0)

    def place(dr, dc):
        return 2 * (dr > 0) + (dc > 0)

    halo = []
    for i, (dr, dc) in enumerate(around):
        if dc == 0:
            src, dst = tok.at[slice(0, 3) if dr < 0 else slice(RL - 3, RL)], rx_rows.at[place(dr, 0) // 2]
        elif dr == 0:
            src, dst = tx_cols.at[place(0, dc)], rx_cols.at[place(0, dc)]
        else:
            src, dst = tx_corner.at[place(dr, dc)], rx_corner.at[place(dr, dc)]
        copy = pltpu.make_async_remote_copy(
            src, dst, h_send.at[i], h_recv.at[i], device_id=beside(dr, dc), device_id_type=MESH
        )
        halo.append((copy, dst, exists(dr, dc), exists(-dr, -dc)))
    for copy, _, to, _ in halo[0:2]:
        pl.when(to)(copy.start)
    for k, csl in enumerate((slice(0, 4), slice(CL - 4, CL))):
        for n, rsl in enumerate((slice(0, 3), slice(RL - 3, RL))):
            tx_corner[2 * n + k] = packed(tok[rsl].astype(F32)[:, csl])
        tx_cols[k] = packed(tok[...].astype(F32)[:, csl])
    for copy, _, to, _ in halo[2:]:
        pl.when(to)(copy.start)

    for fetch in fetches[1:]:
        fetch.wait()
    dk_ext[...] = jnp.zeros_like(dk_ext)
    dv_ext[...] = jnp.zeros_like(dv_ext)
    u_ext[...] = jnp.zeros_like(u_ext)
    gains = gain[...]

    def keyval(unit):
        return dot((unit * gains).astype(BF16), wqkv[:, C : 3 * C])

    x = tok[...].astype(F32).reshape(RL * CL, C)
    unit = x * inverse_rms(x)
    normed = (unit * gains).astype(BF16)
    u_ext[3 : RL + 3, 4 : CL + 4, :] = unit.reshape(RL, CL, C)
    projected = dot(normed, wqkv[...])
    q_loc[...] = (projected[:, 0:C] * 0.125).reshape(RL, CL, C)
    k_ext[3 : RL + 3, 4 : CL + 4, :] = projected[:, C : 2 * C].reshape(RL, CL, C)
    v_ext[3 : RL + 3, 4 : CL + 4, :] = projected[:, 2 * C : 3 * C].reshape(RL, CL, C)
    da_loc[...] = dot(cot[...].reshape(RL * CL, C), wout[...], NT).reshape(RL, CL, C)

    head0 = lax.broadcasted_iota(jnp.int32, (1, C), 1) < 64

    def two_heads(v):
        v = v.astype(BF16)
        zero = jnp.zeros_like(v)
        return jnp.concatenate([jnp.where(head0, v, zero), jnp.where(head0, zero, v)], axis=0)

    def blocks(places):
        each = []
        for row0, nr, col0, nc in places:
            kr, kc, nq = nr + 6, nc + 8, nr * nc
            keys = (slice(row0, row0 + kr), slice(col0, col0 + kc))
            own_at = (slice(row0, row0 + nr), slice(col0, col0 + nc))
            each.append((row0, nr, col0, nc, kr, kc, nq, keys, own_at))
        kws = [k_ext[b[7][0], b[7][1], :].reshape(b[4] * b[5], C).astype(BF16) for b in each]
        vws = [v_ext[b[7][0], b[7][1], :].reshape(b[4] * b[5], C).astype(BF16) for b in each]
        qbs = [two_heads(q_loc[b[8][0], b[8][1], :].reshape(b[6], C)) for b in each]
        dbs = [two_heads(da_loc[b[8][0], b[8][1], :].reshape(b[6], C)) for b in each]
        scores = [dot(kw, qb, NT) for kw, qb in zip(kws, qbs)]
        d_shares = [dot(vw, db, NT) for vw, db in zip(vws, dbs)]
        shares, lows = [], []
        for (row0, nr, col0, nc, kr, kc, nq, _, _), score in zip(each, scores):
            lanes = 2 * nq
            at = lax.broadcasted_iota(jnp.int32, (1, 1, lanes), 2) % nq
            q_row, q_col = at // nc, at % nc
            key_row = lax.broadcasted_iota(jnp.int32, (kr, 1, lanes), 0)
            key_col = lax.broadcasted_iota(jnp.int32, (1, kc, lanes), 1)
            image_row = gx * RL + row0 - 3 + key_row
            image_col = gy * CL + col0 - 4 + key_col
            row_bias = jnp.where(
                (key_row >= q_row) & (key_row <= q_row + 6) & (image_row >= 0) & (image_row < gxn * RL), 0.0, NEG
            )
            col_bias = jnp.where(
                (key_col >= q_col + 1) & (key_col <= q_col + 7) & (image_col >= 0) & (image_col < gyn * CL), 0.0, NEG
            )
            weights = jnp.exp(score.reshape(kr, kc, lanes) + row_bias + col_bias).reshape(kr * kc, lanes)
            totals = jnp.sum(weights, axis=0, keepdims=True)
            shares.append(weights * (1.0 / totals))
            lows.append(shares[-1].astype(BF16))
        a2s = [dot(low, vw, TN) for low, vw in zip(lows, vws)]
        dvs = [dot(low, db) for low, db in zip(lows, dbs)]
        d_scores = []
        for share, d_share in zip(shares, d_shares):
            delta = jnp.sum(share * d_share, axis=0, keepdims=True)
            d_scores.append((share * (d_share - delta)).astype(BF16))
        dq2s = [dot(ds, kw, TN) for ds, kw in zip(d_scores, kws)]
        dks = [dot(ds, qb) for ds, qb in zip(d_scores, qbs)]
        for b, a2, dq2, dk, dv in zip(each, a2s, dq2s, dks, dvs):
            _, nr, _, nc, kr, kc, nq, keys, own_at = b
            att[own_at[0], own_at[1], :] = jnp.where(head0, a2[0:nq], a2[nq:]).reshape(nr, nc, C)
            dq[own_at[0], own_at[1], :] = jnp.where(head0, dq2[0:nq], dq2[nq:]).reshape(nr, nc, C)
            dk_ext[keys[0], keys[1], :] += dk.reshape(kr, kc, C)
            dv_ext[keys[0], keys[1], :] += dv.reshape(kr, kc, C)

    for j in range(1, NB - 1, 2):
        blocks([(3, RL - 6, j * 8, 8), (3, RL - 6, j * 8 + 8, 8)])

    for copy, dst, _, come in halo:
        pl.when(come)(copy.wait_recv)

        @pl.when(jnp.logical_not(come))
        def _():
            dst[...] = jnp.zeros(dst.shape, BF16)

    above, below = slice(0, 3), slice(RL + 3, RE)
    level, far_left, far_right = slice(3, RL + 3), slice(0, 4), slice(CL + 4, CE)
    inside = slice(4, CL + 4)
    rims = (
        (rx_rows[1].reshape(-1, C), above, inside),
        (rx_rows[0].reshape(-1, C), below, inside),
        (rx_cols[1], level, far_left),
        (rx_cols[0], level, far_right),
        (rx_corner[3], above, far_left),
        (rx_corner[2], above, far_right),
        (rx_corner[1], below, far_left),
        (rx_corner[0], below, far_right),
    )
    xh = jnp.concatenate([rim[0].astype(F32) for rim in rims], axis=0)
    uh = xh * inverse_rms(xh)
    kvh = keyval(uh)
    start = 0
    for tokens, rsl, csl in rims:
        n = tokens.shape[0]
        for ref, v in ((u_ext, uh), (k_ext, kvh[:, 0:C]), (v_ext, kvh[:, C:])):
            piece = v[start : start + n]
            piece = piece.reshape(3, CL, C) if csl is inside else unpacked(piece)
            ref[rsl, csl, :] = piece[0 : rsl.stop - rsl.start]
        start += n

    edge = [(3, RL - 6, 0, 8), (3, RL - 6, CL - 8, 8)]
    for col0 in range(0, CL, STRIP):
        edge += [(0, 3, col0, STRIP), (RL - 3, 3, col0, STRIP)]
    blocks(edge[0:5])
    blocks(edge[5:10])

    attended = att[...].reshape(RL * CL, C).astype(BF16)
    d_query = (dq[...] * 0.125).reshape(RL * CL, C).astype(BF16)
    cot_rows = cot[...].reshape(RL * CL, C)
    u = u_ext[...].reshape(RE * CE, C).astype(BF16)
    d_kv = jnp.concatenate(
        [dk_ext[...].reshape(RE * CE, C).astype(BF16), dv_ext[...].reshape(RE * CE, C).astype(BF16)], axis=-1
    )
    g_kv = dot(u, d_kv, TN)
    gsum[0:C, :] = dot(unit.astype(BF16), d_query, TN)
    gsum[C : 2 * C, :] = g_kv[:, 0:C]
    gsum[2 * C : 3 * C, :] = g_kv[:, C : 2 * C]
    gsum[3 * C : 4 * C, :] = dot(attended, cot_rows, TN)
    g16[...] = gsum[...].astype(BF16)
    bases = [lax.rem(y + d, yn) * gyn for d in range(yn)]
    for i, (dy, dc) in enumerate(plane):
        m = bases[dy] + cs[dc]
        pltpu.make_async_remote_copy(
            g16.at[pl.ds(pl.multiple_of(m * rows, rows), rows)],
            rs_rx.at[pl.ds(i * rows, rows)],
            a_send.at[0], a_recv.at[0], device_id=(ys[dy], cs[dc]), device_id_type=MESH,
        ).start()

    dn_ext[...] = dot(d_kv, wqkv[:, C : 3 * C], NT).reshape(RE, CE, C)
    for i, rsl in enumerate((above, below)):
        tx2_rows[i] = dn_ext[rsl, 4 : CL + 4, :].astype(BF16)
        for k, csl in enumerate((far_left, far_right)):
            tx2_corner[2 * i + k] = packed(dn_ext[rsl, csl, :])
    for k, csl in enumerate((far_left, far_right)):
        tx2_cols[k] = packed(dn_ext[level, csl, :])
    back = []
    for i, (dr, dc) in enumerate(around):
        if dc == 0:
            src, dst = tx2_rows.at[place(dr, 0) // 2], rx2_rows.at[place(dr, 0) // 2]
        elif dr == 0:
            src, dst = tx2_cols.at[place(0, dc)], rx2_cols.at[place(0, dc)]
        else:
            src, dst = tx2_corner.at[place(dr, dc)], rx2_corner.at[place(dr, dc)]
        copy = pltpu.make_async_remote_copy(
            src, dst, d_send.at[i], d_recv.at[i], device_id=beside(dr, dc), device_id_type=MESH
        )
        copy.start()
        back.append(copy)

    x = tok[...].astype(F32).reshape(RL * CL, C)
    out[...] = (x + dot(attended, wout[...])).astype(BF16).reshape(RL, CL, C)
    here = pl.ds(pl.multiple_of(me * rows, rows), rows)
    writes = [
        pltpu.make_async_copy(src, dst, out_sem.at[i])
        for i, (src, dst) in enumerate(
            ((out, out_hbm), (tgrad, tgrad_hbm), (own, summed_hbm.at[here]))
        )
    ]
    writes[0].start()
    for copy, _, to, _ in halo:
        pl.when(to)(copy.wait_send)

    wait_bytes(rs_rx, a_recv.at[0])
    mine = gsum[pl.ds(pl.multiple_of(me * rows, rows), rows), :]
    parts = rs_rx[...].astype(F32).reshape(na - 1, rows, C)
    z_rx[pl.ds(z, 1)] = (mine + jnp.sum(parts, axis=0)).astype(BF16)[None]
    for d in column:
        pltpu.make_async_remote_copy(
            z_rx.at[z], z_rx.at[z],
            a_send.at[1], a_recv.at[1], device_id=(zs[d], gy), device_id_type=MESH,
        ).start()

    for copy in back:
        copy.wait()
    first, last = slice(3, 6), slice(RL, RL + 3)
    left, right = slice(4, 8), slice(CL, CL + 4)
    dn_ext[last, inside, :] += rx2_rows[0].astype(F32)
    dn_ext[first, inside, :] += rx2_rows[1].astype(F32)
    dn_ext[level, right, :] += unpacked(rx2_cols[0].astype(F32))
    dn_ext[level, left, :] += unpacked(rx2_cols[1].astype(F32))
    for n, (rsl, csl) in enumerate(((last, right), (last, left), (first, right), (first, left))):
        dn_ext[rsl, csl, :] += unpacked(rx2_corner[n].astype(F32))[0:3]
    d_normed = dot(d_query, wqkv[:, 0:C], NT) + dn_ext[3 : RL + 3, 4 : CL + 4, :].reshape(RL * CL, C)
    x = tok[...].astype(F32).reshape(RL * CL, C)
    r = inverse_rms(x)
    unit = x * r
    g = d_normed * gains
    mean = jnp.sum(g * unit, axis=-1, keepdims=True) * (1.0 / C)
    grads = cot_rows.astype(F32) + r * (g - unit * mean)
    tgrad[...] = grads.astype(BF16).reshape(RL, CL, C)
    writes[1].start()

    wait_bytes(z_rx.at[pl.ds(0, zn - 1)], a_recv.at[1])
    own[...] = jnp.sum(z_rx[...].astype(F32), axis=0).astype(BF16)
    for dy, dc in plane:
        pltpu.make_async_remote_copy(
            own, summed_hbm.at[here],
            a_send.at[2], a_recv.at[2], device_id=(ys[dy], cs[dc]), device_id_type=MESH,
        ).start()
    writes[2].start()
    wait_bytes(z_rx.at[pl.ds(0, zn - 1)], a_send.at[1])
    wait_bytes(rs_rx, a_send.at[0])
    for write in writes:
        write.wait()
    wait_bytes(rs_rx, a_recv.at[2])
    wait_bytes(rs_rx, a_send.at[2])


def finish(
    factor, out, tgrad, summed, gain, wqkv, out_hbm, tgrad_hbm, qkvg_hbm, outg_hbm, gaing_hbm,
    out_v, tgrad_v, summed_v, gain_v, wqkv_v, qkvg, outg, gaing, r_sem, w_sem,
):
    held = ((summed, summed_v), (gain, gain_v), (wqkv, wqkv_v), (out, out_v), (tgrad, tgrad_v))
    reads = [pltpu.make_async_copy(src, dst, r_sem.at[i]) for i, (src, dst) in enumerate(held)]
    made = ((qkvg, qkvg_hbm), (outg, outg_hbm), (gaing, gaing_hbm), (out_v, out_hbm), (tgrad_v, tgrad_hbm))
    writes = [pltpu.make_async_copy(src, dst, w_sem.at[i]) for i, (src, dst) in enumerate(made)]
    for read in reads:
        read.start()
    eye = lax.broadcasted_iota(jnp.int32, (C, C), 0) == lax.broadcasted_iota(jnp.int32, (C, C), 1)
    for read in reads:
        read.wait()
    writes[3].start()
    writes[4].start()
    gain_col = jnp.sum(jnp.where(eye, gain_v[...], 0.0), axis=1, keepdims=True)
    total = jnp.zeros((C, C), F32)
    for i in range(3):
        piece = summed_v[i * C : (i + 1) * C, :].astype(F32) * factor
        qkvg[:, i * C : (i + 1) * C] = piece * gain_col
        total += piece * wqkv_v[:, i * C : (i + 1) * C].astype(F32)
    writes[0].start()
    outg[...] = summed_v[3 * C : 4 * C, :].astype(F32) * factor
    writes[1].start()
    gain_sum = jnp.sum(total, axis=1, keepdims=True)
    gaing[...] = jnp.sum(jnp.where(eye, gain_sum, 0.0), axis=0, keepdims=True)
    writes[2].start()
    for write in writes:
        write.wait()


def per_device(gxn, gyn, zn, tokens, norm_gain, qkv_weight, output_weight, cotangent):
    na = (gxn // zn) * gyn
    rows = 512 // na
    gain_row = norm_gain.reshape(1, C)
    hbm = pl.BlockSpec(memory_space=pl.ANY)
    images = (jax.ShapeDtypeStruct((RL, CL, C), BF16),) * 2
    results = images + (
        jax.ShapeDtypeStruct((C, 3 * C), F32),
        jax.ShapeDtypeStruct((C, C), F32),
        jax.ShapeDtypeStruct((1, C), F32),
    )
    image = pltpu.VMEM((RL, CL, C), BF16)
    image32 = pltpu.VMEM((RL, CL, C), F32)
    ext32 = pltpu.VMEM((RE, CE, C), F32)
    dma = pltpu.SemaphoreType.DMA
    cols = pltpu.VMEM((2, RL * 4, C), BF16)
    corners = pltpu.VMEM((4, 16, C), BF16)
    raw = pl.pallas_call(
        functools.partial(kernel, gxn, gyn, zn),
        out_shape=images + (jax.ShapeDtypeStruct((4 * C, C), BF16),),
        in_specs=[hbm] * 5,
        out_specs=(hbm,) * 3,
        scratch_shapes=[
            image,
            pltpu.VMEM((1, C), F32),
            pltpu.VMEM((C, 3 * C), BF16),
            pltpu.VMEM((C, C), BF16),
            image,
            image,
            image,
            cols,
            corners,
            pltpu.VMEM((2, 3, CL, C), BF16),
            cols,
            corners,
            ext32, ext32, ext32, ext32, ext32, ext32,
            image32, image32, image32, image32,
            pltpu.VMEM((2, 3, CL, C), BF16),
            cols,
            corners,
            pltpu.VMEM((2, 3, CL, C), BF16),
            cols,
            corners,
            pltpu.VMEM((4 * C, C), F32),
            pltpu.VMEM((4 * C, C), BF16),
            pltpu.VMEM(((na - 1) * rows, C), BF16),
            pltpu.VMEM((zn, rows, C), BF16),
            pltpu.VMEM((rows, C), BF16),
            dma((5,)), dma((3,)), dma((8,)), dma((8,)), dma((8,)), dma((8,)), dma((3,)), dma((3,)),
        ],
        compiler_params=pltpu.CompilerParams(
            collective_id=0, has_side_effects=True, vmem_limit_bytes=60 << 20
        ),
    )(
        tokens.reshape(RL, CL, C),
        gain_row,
        qkv_weight,
        output_weight,
        cotangent.reshape(RL, CL, C),
    )
    out, tgrad, qkvg, outg, gaing = pl.pallas_call(
        functools.partial(finish, (gxn * RL * gyn * CL) ** (-0.5)),
        out_shape=results,
        in_specs=[hbm] * 5,
        out_specs=(hbm,) * 5,
        scratch_shapes=[
            image,
            image,
            pltpu.VMEM((4 * C, C), BF16),
            pltpu.VMEM((1, C), F32),
            pltpu.VMEM((C, 3 * C), BF16),
            pltpu.VMEM((C, 3 * C), F32),
            pltpu.VMEM((C, C), F32),
            pltpu.VMEM((1, C), F32),
            dma((5,)),
            dma((5,)),
        ],
        compiler_params=pltpu.CompilerParams(vmem_limit_bytes=60 << 20),
    )(*raw, gain_row, qkv_weight)
    return (
        out.reshape(tokens.shape),
        tgrad.reshape(tokens.shape),
        qkvg,
        outg,
        gaing.reshape(C),
    )


def solution(mesh):
    gxn, gyn = mesh.shape["gx"], mesh.shape["gy"]
    image = P(None, "gx", "gy", None)
    return jax.shard_map(
        functools.partial(per_device, gxn, gyn, min(ZN, max(gxn // 4, 2))),
        mesh=mesh,
        in_specs=(image, P(), P(), P(), image),
        out_specs=(image, image, P(), P(), P()),
        check_vma=False,
    )
```

```python
import functools

import jax
import jax.numpy as jnp
from jax import lax
from jax.experimental import pallas as pl
from jax.experimental.pallas import tpu as pltpu
from jax.sharding import PartitionSpec as P

MESH = pl.DeviceIdType.MESH
EPS = 1e-06
F32 = jnp.float32
BF16 = jnp.bfloat16
C = 128
RL, CL = 16, 64
RE, CE = RL + 6, CL + 8
NB = CL // 8
STRIP = 16
NEG = -1e30
ZN = 8

NT = (((1,), (1,)), ((), ()))
TN = (((0,), (0,)), ((), ()))


def dot(a, b, dims=(((1,), (0,)), ((), ()))):
    return lax.dot_general(a, b, dims, preferred_element_type=F32)


def inverse_rms(x):
    return lax.rsqrt(jnp.sum(x * x, axis=-1, keepdims=True) * (1.0 / C) + EPS)


def kernel(
    gxn, gyn, zn,
    tok_hbm, gain_hbm, wqkv_hbm, wout_hbm, cot_hbm,
    out_hbm, tgrad_hbm, summed_hbm,
    tok, gain, wqkv, wout, cot,
    out, tgrad,
    tx_cols, tx_corner, rx_rows, rx_cols, rx_corner,
    u_ext, k_ext, v_ext, dk_ext, dv_ext, dn_ext,
    q_loc, da_loc, att, dq,
    tx2_rows, tx2_cols, tx2_corner, rx2_rows, rx2_cols, rx2_corner,
    gsum, g16, rs_rx, z_rx, own,
    in_sem, out_sem, h_send, h_recv, d_send, d_recv, a_send, a_recv,
):
    yn = gxn // zn
    na = yn * gyn
    rows = 512 // na
    gx = lax.axis_index("gx")
    gy = lax.axis_index("gy")
    y, z = lax.div(gx, zn), lax.rem(gx, zn)
    me = y * gyn + gy
    ys = [lax.rem(y + d, yn) * zn + z for d in range(yn)]
    cs = [lax.rem(gy + d, gyn) for d in range(gyn)]
    zs = [y * zn + lax.rem(z + d, zn) for d in range(zn)]

    def far(d, n):
        return min(d, n - d)

    plane = sorted(
        ((dy, dc) for dy in range(yn) for dc in range(gyn) if dy or dc),
        key=lambda o: (-far(o[0], yn) - far(o[1], gyn) / 2, o),
    )
    column = sorted(range(1, zn), key=lambda d: (-far(d, zn), d))

    def beside(dr, dc):
        return (lax.rem(gx + (dr + gxn), gxn) if dr else gx, cs[dc % gyn])

    def exists(dr, dc):
        r, c = gx + dr, gy + dc
        return (r >= 0) & (r < gxn) & (c >= 0) & (c < gyn)

    def wait_bytes(ref, sem):
        pltpu.make_async_copy(ref, ref, sem).wait()

    fetches = [
        pltpu.make_async_copy(src, dst, in_sem.at[i])
        for i, (src, dst) in enumerate(
            ((tok_hbm, tok), (gain_hbm, gain), (wqkv_hbm, wqkv), (cot_hbm, cot), (wout_hbm, wout))
        )
    ]
    around = [(-1, 0), (1, 0), (-1, -1), (-1, 1), (1, -1), (1, 1), (0, -1), (0, 1)]
    barrier = pltpu.get_barrier_semaphore()

    def greet(device):
        pl.semaphore_signal(barrier, inc=1, device_id=device, device_id_type=MESH)

    for fetch in fetches:
        fetch.start()
    for d in column:
        greet((zs[d], gy))
    for dy, dc in plane:
        greet((ys[dy], cs[dc]))
    for dr, dc in around:
        if dr:
            greet(beside(dr, dc))
    fetches[0].wait()
    pl.semaphore_wait(barrier, 6 + (zn - 1) + (na - 1))

    def packed(v):
        if v.shape[0] == 3:
            v = jnp.concatenate([v, v[0:1]], axis=0)
        half = v.shape[0] // 2
        return jnp.concatenate([v[0:half], v[half:]], axis=1).reshape(half * 8, C).astype(BF16)

    def unpacked(v):
        v = v.reshape(-1, 8, C)
        return jnp.concatenate([v[:, 0:4], v[:, 4:8]], axis=0)

    def place(dr, dc):
        return 2 * (dr > 0) + (dc > 0)

    halo = []
    for i, (dr, dc) in enumerate(around):
        if dc == 0:
            src, dst = tok.at[slice(0, 3) if dr < 0 else slice(RL - 3, RL)], rx_rows.at[place(dr, 0) // 2]
        elif dr == 0:
            src, dst = tx_cols.at[place(0, dc)], rx_cols.at[place(0, dc)]
        else:
            src, dst = tx_corner.at[place(dr, dc)], rx_corner.at[place(dr, dc)]
        copy = pltpu.make_async_remote_copy(
            src, dst, h_send.at[i], h_recv.at[i], device_id=beside(dr, dc), device_id_type=MESH
        )
        halo.append((copy, dst, exists(dr, dc), exists(-dr, -dc)))
    for copy, _, to, _ in halo[0:2]:
        pl.when(to)(copy.start)
    for k, csl in enumerate((slice(0, 4), slice(CL - 4, CL))):
        for n, rsl in enumerate((slice(0, 3), slice(RL - 3, RL))):
            tx_corner[2 * n + k] = packed(tok[rsl].astype(F32)[:, csl])
        tx_cols[k] = packed(tok[...].astype(F32)[:, csl])
    for copy, _, to, _ in halo[2:]:
        pl.when(to)(copy.start)

    for fetch in fetches[1:]:
        fetch.wait()
    dk_ext[...] = jnp.zeros_like(dk_ext)
    dv_ext[...] = jnp.zeros_like(dv_ext)
    u_ext[...] = jnp.zeros_like(u_ext)
    gains = gain[...]

    def keyval(unit):
        return dot((unit * gains).astype(BF16), wqkv[:, C : 3 * C])

    x = tok[...].astype(F32).reshape(RL * CL, C)
    unit = x * inverse_rms(x)
    normed = (unit * gains).astype(BF16)
    u_ext[3 : RL + 3, 4 : CL + 4, :] = unit.reshape(RL, CL, C)
    projected = dot(normed, wqkv[...])
    q_loc[...] = (projected[:, 0:C] * 0.125).reshape(RL, CL, C)
    k_ext[3 : RL + 3, 4 : CL + 4, :] = projected[:, C : 2 * C].reshape(RL, CL, C)
    v_ext[3 : RL + 3, 4 : CL + 4, :] = projected[:, 2 * C : 3 * C].reshape(RL, CL, C)
    da_loc[...] = dot(cot[...].reshape(RL * CL, C), wout[...], NT).reshape(RL, CL, C)

    head0 = lax.broadcasted_iota(jnp.int32, (1, C), 1) < 64

    def two_heads(v):
        v = v.astype(BF16)
        zero = jnp.zeros_like(v)
        return jnp.concatenate([jnp.where(head0, v, zero), jnp.where(head0, zero, v)], axis=0)

    def blocks(places):
        each = []
        for row0, nr, col0, nc in places:
            kr, kc, nq = nr + 6, nc + 8, nr * nc
            keys = (slice(row0, row0 + kr), slice(col0, col0 + kc))
            own_at = (slice(row0, row0 + nr), slice(col0, col0 + nc))
            each.append((row0, nr, col0, nc, kr, kc, nq, keys, own_at))
        kws = [k_ext[b[7][0], b[7][1], :].reshape(b[4] * b[5], C).astype(BF16) for b in each]
        vws = [v_ext[b[7][0], b[7][1], :].reshape(b[4] * b[5], C).astype(BF16) for b in each]
        qbs = [two_heads(q_loc[b[8][0], b[8][1], :].reshape(b[6], C)) for b in each]
        dbs = [two_heads(da_loc[b[8][0], b[8][1], :].reshape(b[6], C)) for b in each]
        scores = [dot(kw, qb, NT) for kw, qb in zip(kws, qbs)]
        d_shares = [dot(vw, db, NT) for vw, db in zip(vws, dbs)]
        shares, lows = [], []
        for (row0, nr, col0, nc, kr, kc, nq, _, _), score in zip(each, scores):
            lanes = 2 * nq
            at = lax.broadcasted_iota(jnp.int32, (1, 1, lanes), 2) % nq
            q_row, q_col = at // nc, at % nc
            key_row = lax.broadcasted_iota(jnp.int32, (kr, 1, lanes), 0)
            key_col = lax.broadcasted_iota(jnp.int32, (1, kc, lanes), 1)
            image_row = gx * RL + row0 - 3 + key_row
            image_col = gy * CL + col0 - 4 + key_col
            row_bias = jnp.where(
                (key_row >= q_row) & (key_row <= q_row + 6) & (image_row >= 0) & (image_row < gxn * RL), 0.0, NEG
            )
            col_bias = jnp.where(
                (key_col >= q_col + 1) & (key_col <= q_col + 7) & (image_col >= 0) & (image_col < gyn * CL), 0.0, NEG
            )
            weights = jnp.exp(score.reshape(kr, kc, lanes) + row_bias + col_bias).reshape(kr * kc, lanes)
            totals = jnp.sum(weights, axis=0, keepdims=True)
            shares.append(weights * (1.0 / totals))
            lows.append(shares[-1].astype(BF16))
        a2s = [dot(low, vw, TN) for low, vw in zip(lows, vws)]
        dvs = [dot(low, db) for low, db in zip(lows, dbs)]
        d_scores = []
        for share, d_share in zip(shares, d_shares):
            delta = jnp.sum(share * d_share, axis=0, keepdims=True)
            d_scores.append((share * (d_share - delta)).astype(BF16))
        dq2s = [dot(ds, kw, TN) for ds, kw in zip(d_scores, kws)]
        dks = [dot(ds, qb) for ds, qb in zip(d_scores, qbs)]
        for b, a2, dq2, dk, dv in zip(each, a2s, dq2s, dks, dvs):
            _, nr, _, nc, kr, kc, nq, keys, own_at = b
            att[own_at[0], own_at[1], :] = jnp.where(head0, a2[0:nq], a2[nq:]).reshape(nr, nc, C)
            dq[own_at[0], own_at[1], :] = jnp.where(head0, dq2[0:nq], dq2[nq:]).reshape(nr, nc, C)
            dk_ext[keys[0], keys[1], :] += dk.reshape(kr, kc, C)
            dv_ext[keys[0], keys[1], :] += dv.reshape(kr, kc, C)

    for j in range(1, NB - 1, 2):
        blocks([(3, RL - 6, j * 8, 8), (3, RL - 6, j * 8 + 8, 8)])

    for copy, dst, _, come in halo:
        pl.when(come)(copy.wait_recv)

    above, below = slice(0, 3), slice(RL + 3, RE)
    level, far_left, far_right = slice(3, RL + 3), slice(0, 4), slice(CL + 4, CE)
    inside = slice(4, CL + 4)
    rims = (
        (rx_rows[1].reshape(-1, C), above, inside),
        (rx_rows[0].reshape(-1, C), below, inside),
        (rx_cols[1], level, far_left),
        (rx_cols[0], level, far_right),
        (rx_corner[3], above, far_left),
        (rx_corner[2], above, far_right),
        (rx_corner[1], below, far_left),
        (rx_corner[0], below, far_right),
    )
    has = ((-1, 0), (1, 0), (0, -1), (0, 1), (-1, -1), (-1, 1), (1, -1), (1, 1))
    xh = jnp.concatenate(
        [jnp.where(exists(dr, dc), rim[0].astype(F32), 0.0) for rim, (dr, dc) in zip(rims, has)], axis=0
    )
    uh = xh * inverse_rms(xh)
    kvh = keyval(uh)
    start = 0
    for tokens, rsl, csl in rims:
        n = tokens.shape[0]
        for ref, v in ((u_ext, uh), (k_ext, kvh[:, 0:C]), (v_ext, kvh[:, C:])):
            piece = v[start : start + n]
            piece = piece.reshape(3, CL, C) if csl is inside else unpacked(piece)
            ref[rsl, csl, :] = piece[0 : rsl.stop - rsl.start]
        start += n

    edge = [(3, RL - 6, 0, 8), (3, RL - 6, CL - 8, 8)]
    for col0 in range(0, CL, STRIP):
        edge += [(0, 3, col0, STRIP), (RL - 3, 3, col0, STRIP)]
    blocks(edge[0:5])
    blocks(edge[5:10])

    attended = att[...].reshape(RL * CL, C).astype(BF16)
    d_query = (dq[...] * 0.125).reshape(RL * CL, C).astype(BF16)
    cot_rows = cot[...].reshape(RL * CL, C)
    u = u_ext[...].reshape(RE * CE, C).astype(BF16)
    d_kv = jnp.concatenate(
        [dk_ext[...].reshape(RE * CE, C).astype(BF16), dv_ext[...].reshape(RE * CE, C).astype(BF16)], axis=-1
    )
    g_kv = dot(u, d_kv, TN)
    gsum[0:C, :] = dot(unit.astype(BF16), d_query, TN)
    gsum[C : 2 * C, :] = g_kv[:, 0:C]
    gsum[2 * C : 3 * C, :] = g_kv[:, C : 2 * C]
    gsum[3 * C : 4 * C, :] = dot(attended, cot_rows, TN)
    g16[...] = gsum[...].astype(BF16)
    bases = [lax.rem(y + d, yn) * gyn for d in range(yn)]
    for i, (dy, dc) in enumerate(plane):
        m = bases[dy] + cs[dc]
        pltpu.make_async_remote_copy(
            g16.at[pl.ds(pl.multiple_of(m * rows, rows), rows)],
            rs_rx.at[pl.ds(i * rows, rows)],
            a_send.at[0], a_recv.at[0], device_id=(ys[dy], cs[dc]), device_id_type=MESH,
        ).start()

    dn_ext[...] = dot(d_kv, wqkv[:, C : 3 * C], NT).reshape(RE, CE, C)
    for i, rsl in enumerate((above, below)):
        tx2_rows[i] = dn_ext[rsl, 4 : CL + 4, :].astype(BF16)
        for k, csl in enumerate((far_left, far_right)):
            tx2_corner[2 * i + k] = packed(dn_ext[rsl, csl, :])
    for k, csl in enumerate((far_left, far_right)):
        tx2_cols[k] = packed(dn_ext[level, csl, :])
    back = []
    for i, (dr, dc) in enumerate(around):
        if dc == 0:
            src, dst = tx2_rows.at[place(dr, 0) // 2], rx2_rows.at[place(dr, 0) // 2]
        elif dr == 0:
            src, dst = tx2_cols.at[place(0, dc)], rx2_cols.at[place(0, dc)]
        else:
            src, dst = tx2_corner.at[place(dr, dc)], rx2_corner.at[place(dr, dc)]
        copy = pltpu.make_async_remote_copy(
            src, dst, d_send.at[i], d_recv.at[i], device_id=beside(dr, dc), device_id_type=MESH
        )
        copy.start()
        back.append(copy)

    x = tok[...].astype(F32).reshape(RL * CL, C)
    out[...] = (x + dot(attended, wout[...])).astype(BF16).reshape(RL, CL, C)
    here = pl.ds(pl.multiple_of(me * rows, rows), rows)
    writes = [
        pltpu.make_async_copy(src, dst, out_sem.at[i])
        for i, (src, dst) in enumerate(
            ((out, out_hbm), (tgrad, tgrad_hbm), (own, summed_hbm.at[here]))
        )
    ]
    writes[0].start()
    for copy, _, to, _ in halo:
        pl.when(to)(copy.wait_send)

    wait_bytes(rs_rx, a_recv.at[0])
    mine = gsum[pl.ds(pl.multiple_of(me * rows, rows), rows), :]
    parts = rs_rx[...].astype(F32).reshape(na - 1, rows, C)
    z_rx[pl.ds(z, 1)] = (mine + jnp.sum(parts, axis=0)).astype(BF16)[None]
    for d in column:
        pltpu.make_async_remote_copy(
            z_rx.at[z], z_rx.at[z],
            a_send.at[1], a_recv.at[1], device_id=(zs[d], gy), device_id_type=MESH,
        ).start()

    for copy in back:
        copy.wait()
    first, last = slice(3, 6), slice(RL, RL + 3)
    left, right = slice(4, 8), slice(CL, CL + 4)
    dn_ext[last, inside, :] += rx2_rows[0].astype(F32)
    dn_ext[first, inside, :] += rx2_rows[1].astype(F32)
    dn_ext[level, right, :] += unpacked(rx2_cols[0].astype(F32))
    dn_ext[level, left, :] += unpacked(rx2_cols[1].astype(F32))
    for n, (rsl, csl) in enumerate(((last, right), (last, left), (first, right), (first, left))):
        dn_ext[rsl, csl, :] += unpacked(rx2_corner[n].astype(F32))[0:3]
    d_normed = dot(d_query, wqkv[:, 0:C], NT) + dn_ext[3 : RL + 3, 4 : CL + 4, :].reshape(RL * CL, C)
    x = tok[...].astype(F32).reshape(RL * CL, C)
    r = inverse_rms(x)
    unit = x * r
    g = d_normed * gains
    mean = jnp.sum(g * unit, axis=-1, keepdims=True) * (1.0 / C)
    grads = cot_rows.astype(F32) + r * (g - unit * mean)
    tgrad[...] = grads.astype(BF16).reshape(RL, CL, C)
    writes[1].start()

    wait_bytes(z_rx.at[pl.ds(0, zn - 1)], a_recv.at[1])
    own[...] = jnp.sum(z_rx[...].astype(F32), axis=0).astype(BF16)
    for dy, dc in plane:
        pltpu.make_async_remote_copy(
            own, summed_hbm.at[here],
            a_send.at[2], a_recv.at[2], device_id=(ys[dy], cs[dc]), device_id_type=MESH,
        ).start()
    writes[2].start()
    wait_bytes(z_rx.at[pl.ds(0, zn - 1)], a_send.at[1])
    wait_bytes(rs_rx, a_send.at[0])
    for write in writes:
        write.wait()
    wait_bytes(rs_rx, a_recv.at[2])
    wait_bytes(rs_rx, a_send.at[2])


def finish(
    factor, out, tgrad, summed, gain, wqkv, out_hbm, tgrad_hbm, qkvg_hbm, outg_hbm, gaing_hbm,
    out_v, tgrad_v, summed_v, gain_v, wqkv_v, qkvg, outg, gaing, r_sem, w_sem,
):
    held = ((summed, summed_v), (gain, gain_v), (wqkv, wqkv_v), (out, out_v), (tgrad, tgrad_v))
    reads = [pltpu.make_async_copy(src, dst, r_sem.at[i]) for i, (src, dst) in enumerate(held)]
    made = ((qkvg, qkvg_hbm), (outg, outg_hbm), (gaing, gaing_hbm), (out_v, out_hbm), (tgrad_v, tgrad_hbm))
    writes = [pltpu.make_async_copy(src, dst, w_sem.at[i]) for i, (src, dst) in enumerate(made)]
    for read in reads:
        read.start()
    eye = lax.broadcasted_iota(jnp.int32, (C, C), 0) == lax.broadcasted_iota(jnp.int32, (C, C), 1)
    reads[1].wait()
    gain_col = jnp.sum(jnp.where(eye, gain_v[...], 0.0), axis=1, keepdims=True) * factor
    reads[0].wait()
    reads[2].wait()
    outg[...] = summed_v[3 * C : 4 * C, :].astype(F32) * factor
    writes[1].start()
    total = jnp.zeros((C, C), F32)
    for i in range(3):
        piece = summed_v[i * C : (i + 1) * C, :].astype(F32)
        qkvg[:, i * C : (i + 1) * C] = piece * gain_col
        total += piece * wqkv_v[:, i * C : (i + 1) * C].astype(F32)
    writes[0].start()
    for i in (3, 4):
        reads[i].wait()
        writes[i].start()
    gain_sum = jnp.sum(total, axis=1, keepdims=True) * factor
    gaing[...] = jnp.sum(jnp.where(eye, gain_sum, 0.0), axis=0, keepdims=True)
    writes[2].start()
    for write in writes:
        write.wait()


def per_device(gxn, gyn, zn, tokens, norm_gain, qkv_weight, output_weight, cotangent):
    na = (gxn // zn) * gyn
    rows = 512 // na
    gain_row = norm_gain.reshape(1, C)
    hbm = pl.BlockSpec(memory_space=pl.ANY)
    images = (jax.ShapeDtypeStruct((RL, CL, C), BF16),) * 2
    results = images + (
        jax.ShapeDtypeStruct((C, 3 * C), F32),
        jax.ShapeDtypeStruct((C, C), F32),
        jax.ShapeDtypeStruct((1, C), F32),
    )
    image = pltpu.VMEM((RL, CL, C), BF16)
    image32 = pltpu.VMEM((RL, CL, C), F32)
    ext32 = pltpu.VMEM((RE, CE, C), F32)
    dma = pltpu.SemaphoreType.DMA
    cols = pltpu.VMEM((2, RL * 4, C), BF16)
    corners = pltpu.VMEM((4, 16, C), BF16)
    raw = pl.pallas_call(
        functools.partial(kernel, gxn, gyn, zn),
        out_shape=images + (jax.ShapeDtypeStruct((4 * C, C), BF16),),
        in_specs=[hbm] * 5,
        out_specs=(hbm,) * 3,
        scratch_shapes=[
            image,
            pltpu.VMEM((1, C), F32),
            pltpu.VMEM((C, 3 * C), BF16),
            pltpu.VMEM((C, C), BF16),
            image,
            image,
            image,
            cols,
            corners,
            pltpu.VMEM((2, 3, CL, C), BF16),
            cols,
            corners,
            ext32, ext32, ext32, ext32, ext32, ext32,
            image32, image32, image32, image32,
            pltpu.VMEM((2, 3, CL, C), BF16),
            cols,
            corners,
            pltpu.VMEM((2, 3, CL, C), BF16),
            cols,
            corners,
            pltpu.VMEM((4 * C, C), F32),
            pltpu.VMEM((4 * C, C), BF16),
            pltpu.VMEM(((na - 1) * rows, C), BF16),
            pltpu.VMEM((zn, rows, C), BF16),
            pltpu.VMEM((rows, C), BF16),
            dma((5,)), dma((3,)), dma((8,)), dma((8,)), dma((8,)), dma((8,)), dma((3,)), dma((3,)),
        ],
        compiler_params=pltpu.CompilerParams(
            collective_id=0, has_side_effects=True, vmem_limit_bytes=60 << 20
        ),
    )(
        tokens.reshape(RL, CL, C),
        gain_row,
        qkv_weight,
        output_weight,
        cotangent.reshape(RL, CL, C),
    )
    out, tgrad, qkvg, outg, gaing = pl.pallas_call(
        functools.partial(finish, (gxn * RL * gyn * CL) ** (-0.5)),
        out_shape=results,
        in_specs=[hbm] * 5,
        out_specs=(hbm,) * 5,
        scratch_shapes=[
            image,
            image,
            pltpu.VMEM((4 * C, C), BF16),
            pltpu.VMEM((1, C), F32),
            pltpu.VMEM((C, 3 * C), BF16),
            pltpu.VMEM((C, 3 * C), F32),
            pltpu.VMEM((C, C), F32),
            pltpu.VMEM((1, C), F32),
            dma((5,)),
            dma((5,)),
        ],
        compiler_params=pltpu.CompilerParams(vmem_limit_bytes=60 << 20),
    )(*raw, gain_row, qkv_weight)
    return (
        out.reshape(tokens.shape),
        tgrad.reshape(tokens.shape),
        qkvg,
        outg,
        gaing.reshape(C),
    )


def solution(mesh):
    gxn, gyn = mesh.shape["gx"], mesh.shape["gy"]
    image = P(None, "gx", "gy", None)
    return jax.shard_map(
        functools.partial(per_device, gxn, gyn, min(ZN, max(gxn // 4, 2))),
        mesh=mesh,
        in_specs=(image, P(), P(), P(), image),
        out_specs=(image, image, P(), P(), P()),
        check_vma=False,
    )
```

```python
import functools

import jax
import jax.numpy as jnp
from jax import lax
from jax.experimental import pallas as pl
from jax.experimental.pallas import tpu as pltpu
from jax.sharding import PartitionSpec as P

MESH = pl.DeviceIdType.MESH
EPS = 1e-06
F32 = jnp.float32
BF16 = jnp.bfloat16
C = 128
RL, CL = 16, 64
RE, CE = RL + 6, CL + 8
NB = CL // 8
STRIP = 16
NEG = -1e30
ZN = 8

NT = (((1,), (1,)), ((), ()))
TN = (((0,), (0,)), ((), ()))


def dot(a, b, dims=(((1,), (0,)), ((), ()))):
    return lax.dot_general(a, b, dims, preferred_element_type=F32)


def inverse_rms(x):
    return lax.rsqrt(jnp.sum(x * x, axis=-1, keepdims=True) * (1.0 / C) + EPS)


def kernel(
    gxn, gyn, zn,
    tok_hbm, gain_hbm, wqkv_hbm, wout_hbm, cot_hbm,
    out_hbm, tgrad_hbm, summed_hbm,
    tok, gain, wqkv, wout, cot,
    out, tgrad,
    tx_cols, tx_corner, rx_rows, rx_cols, rx_corner,
    u_ext, k_ext, v_ext, dk_ext, dv_ext, dn_ext,
    q_loc, da_loc, att, dq,
    tx2_rows, tx2_cols, tx2_corner, rx2_rows, rx2_cols, rx2_corner,
    gsum, g16, rs_rx, z_rx, own,
    in_sem, out_sem, h_send, h_recv, d_send, d_recv, a_send, a_recv,
):
    yn = gxn // zn
    na = yn * gyn
    rows = 512 // na
    gx = lax.axis_index("gx")
    gy = lax.axis_index("gy")
    y, z = lax.div(gx, zn), lax.rem(gx, zn)
    me = y * gyn + gy
    ys = [lax.rem(y + d, yn) * zn + z for d in range(yn)]
    cs = [lax.rem(gy + d, gyn) for d in range(gyn)]
    zs = [y * zn + lax.rem(z + d, zn) for d in range(zn)]

    def far(d, n):
        return min(d, n - d)

    plane = sorted(
        ((dy, dc) for dy in range(yn) for dc in range(gyn) if dy or dc),
        key=lambda o: (-far(o[0], yn) - far(o[1], gyn) / 2, o),
    )
    column = sorted(range(1, zn), key=lambda d: (-far(d, zn), d))

    def beside(dr, dc):
        return (lax.rem(gx + (dr + gxn), gxn) if dr else gx, cs[dc % gyn])

    def exists(dr, dc):
        r, c = gx + dr, gy + dc
        return (r >= 0) & (r < gxn) & (c >= 0) & (c < gyn)

    def wait_bytes(ref, sem):
        pltpu.make_async_copy(ref, ref, sem).wait()

    fetches = [
        pltpu.make_async_copy(src, dst, in_sem.at[i])
        for i, (src, dst) in enumerate(
            ((tok_hbm, tok), (gain_hbm, gain), (wqkv_hbm, wqkv), (cot_hbm, cot), (wout_hbm, wout))
        )
    ]
    around = [(-1, 0), (1, 0), (-1, -1), (-1, 1), (1, -1), (1, 1), (0, -1), (0, 1)]
    barrier = pltpu.get_barrier_semaphore()

    def greet(device):
        pl.semaphore_signal(barrier, inc=1, device_id=device, device_id_type=MESH)

    for fetch in fetches:
        fetch.start()
    for d in column:
        greet((zs[d], gy))
    for dy, dc in plane:
        greet((ys[dy], cs[dc]))
    for dr, dc in around:
        if dr:
            greet(beside(dr, dc))
    fetches[0].wait()
    pl.semaphore_wait(barrier, 6 + (zn - 1) + (na - 1))

    def packed(v):
        if v.shape[0] == 3:
            v = jnp.concatenate([v, v[0:1]], axis=0)
        half = v.shape[0] // 2
        return jnp.concatenate([v[0:half], v[half:]], axis=1).reshape(half * 8, C).astype(BF16)

    def unpacked(v):
        v = v.reshape(-1, 8, C)
        return jnp.concatenate([v[:, 0:4], v[:, 4:8]], axis=0)

    def place(dr, dc):
        return 2 * (dr > 0) + (dc > 0)

    halo = []
    for i, (dr, dc) in enumerate(around):
        if dc == 0:
            src, dst = tok.at[slice(0, 3) if dr < 0 else slice(RL - 3, RL)], rx_rows.at[place(dr, 0) // 2]
        elif dr == 0:
            src, dst = tx_cols.at[place(0, dc)], rx_cols.at[place(0, dc)]
        else:
            src, dst = tx_corner.at[place(dr, dc)], rx_corner.at[place(dr, dc)]
        copy = pltpu.make_async_remote_copy(
            src, dst, h_send.at[i], h_recv.at[i], device_id=beside(dr, dc), device_id_type=MESH
        )
        halo.append((copy, dst, exists(dr, dc), exists(-dr, -dc)))
    for copy, _, to, _ in halo[0:2]:
        pl.when(to)(copy.start)
    for k, csl in enumerate((slice(0, 4), slice(CL - 4, CL))):
        for n, rsl in enumerate((slice(0, 3), slice(RL - 3, RL))):
            tx_corner[2 * n + k] = packed(tok[rsl].astype(F32)[:, csl])
        tx_cols[k] = packed(tok[...].astype(F32)[:, csl])
    for copy, _, to, _ in halo[2:]:
        pl.when(to)(copy.start)

    for fetch in fetches[1:]:
        fetch.wait()
    dk_ext[...] = jnp.zeros_like(dk_ext)
    dv_ext[...] = jnp.zeros_like(dv_ext)
    u_ext[...] = jnp.zeros_like(u_ext)
    gains = gain[...]

    def keyval(unit):
        return dot((unit * gains).astype(BF16), wqkv[:, C : 3 * C])

    x = tok[...].astype(F32).reshape(RL * CL, C)
    unit = x * inverse_rms(x)
    normed = (unit * gains).astype(BF16)
    u_ext[3 : RL + 3, 4 : CL + 4, :] = unit.reshape(RL, CL, C)
    projected = dot(normed, wqkv[...])
    q_loc[...] = (projected[:, 0:C] * 0.125).reshape(RL, CL, C)
    k_ext[3 : RL + 3, 4 : CL + 4, :] = projected[:, C : 2 * C].reshape(RL, CL, C)
    v_ext[3 : RL + 3, 4 : CL + 4, :] = projected[:, 2 * C : 3 * C].reshape(RL, CL, C)
    da_loc[...] = dot(cot[...].reshape(RL * CL, C), wout[...], NT).reshape(RL, CL, C)

    head0 = lax.broadcasted_iota(jnp.int32, (1, C), 1) < 64

    def two_heads(v):
        v = v.astype(BF16)
        zero = jnp.zeros_like(v)
        return jnp.concatenate([jnp.where(head0, v, zero), jnp.where(head0, zero, v)], axis=0)

    def blocks(places):
        each = []
        for row0, nr, col0, nc in places:
            kr, kc, nq = nr + 6, nc + 8, nr * nc
            keys = (slice(row0, row0 + kr), slice(col0, col0 + kc))
            own_at = (slice(row0, row0 + nr), slice(col0, col0 + nc))
            each.append((row0, nr, col0, nc, kr, kc, nq, keys, own_at))
        kws = [k_ext[b[7][0], b[7][1], :].reshape(b[4] * b[5], C).astype(BF16) for b in each]
        vws = [v_ext[b[7][0], b[7][1], :].reshape(b[4] * b[5], C).astype(BF16) for b in each]
        qbs = [two_heads(q_loc[b[8][0], b[8][1], :].reshape(b[6], C)) for b in each]
        dbs = [two_heads(da_loc[b[8][0], b[8][1], :].reshape(b[6], C)) for b in each]
        scores = [dot(kw, qb, NT) for kw, qb in zip(kws, qbs)]
        d_shares = [dot(vw, db, NT) for vw, db in zip(vws, dbs)]
        shares, lows = [], []
        for (row0, nr, col0, nc, kr, kc, nq, _, _), score in zip(each, scores):
            lanes = 2 * nq
            at = lax.broadcasted_iota(jnp.int32, (1, 1, lanes), 2) % nq
            q_row, q_col = at // nc, at % nc
            key_row = lax.broadcasted_iota(jnp.int32, (kr, 1, lanes), 0)
            key_col = lax.broadcasted_iota(jnp.int32, (1, kc, lanes), 1)
            image_row = gx * RL + row0 - 3 + key_row
            image_col = gy * CL + col0 - 4 + key_col
            row_bias = jnp.where(
                (key_row >= q_row) & (key_row <= q_row + 6) & (image_row >= 0) & (image_row < gxn * RL), 0.0, NEG
            )
            col_bias = jnp.where(
                (key_col >= q_col + 1) & (key_col <= q_col + 7) & (image_col >= 0) & (image_col < gyn * CL), 0.0, NEG
            )
            weights = jnp.exp(score.reshape(kr, kc, lanes) + row_bias + col_bias).reshape(kr * kc, lanes)
            totals = jnp.sum(weights, axis=0, keepdims=True)
            scale = jnp.where(totals > 1.0, 2.0**-64, 1.0)
            shares.append(weights * (1.0 / (totals * scale)) * scale)
            lows.append(shares[-1].astype(BF16))
        a2s = [dot(low, vw, TN) for low, vw in zip(lows, vws)]
        dvs = [dot(low, db) for low, db in zip(lows, dbs)]
        d_scores = []
        for share, d_share in zip(shares, d_shares):
            delta = jnp.sum(share * d_share, axis=0, keepdims=True)
            d_scores.append((share * (d_share - delta)).astype(BF16))
        dq2s = [dot(ds, kw, TN) for ds, kw in zip(d_scores, kws)]
        dks = [dot(ds, qb) for ds, qb in zip(d_scores, qbs)]
        for b, a2, dq2, dk, dv in zip(each, a2s, dq2s, dks, dvs):
            _, nr, _, nc, kr, kc, nq, keys, own_at = b
            att[own_at[0], own_at[1], :] = jnp.where(head0, a2[0:nq], a2[nq:]).reshape(nr, nc, C)
            dq[own_at[0], own_at[1], :] = jnp.where(head0, dq2[0:nq], dq2[nq:]).reshape(nr, nc, C)
            dk_ext[keys[0], keys[1], :] += dk.reshape(kr, kc, C)
            dv_ext[keys[0], keys[1], :] += dv.reshape(kr, kc, C)

    for j in range(1, NB - 1, 2):
        blocks([(3, RL - 6, j * 8, 8), (3, RL - 6, j * 8 + 8, 8)])

    for copy, dst, _, come in halo:
        pl.when(come)(copy.wait_recv)

    above, below = slice(0, 3), slice(RL + 3, RE)
    level, far_left, far_right = slice(3, RL + 3), slice(0, 4), slice(CL + 4, CE)
    inside = slice(4, CL + 4)
    rims = (
        (rx_rows[1].reshape(-1, C), above, inside),
        (rx_rows[0].reshape(-1, C), below, inside),
        (rx_cols[1], level, far_left),
        (rx_cols[0], level, far_right),
        (rx_corner[3], above, far_left),
        (rx_corner[2], above, far_right),
        (rx_corner[1], below, far_left),
        (rx_corner[0], below, far_right),
    )
    has = ((-1, 0), (1, 0), (0, -1), (0, 1), (-1, -1), (-1, 1), (1, -1), (1, 1))
    xh = jnp.concatenate(
        [jnp.where(exists(dr, dc), rim[0].astype(F32), 0.0) for rim, (dr, dc) in zip(rims, has)], axis=0
    )
    uh = xh * inverse_rms(xh)
    kvh = keyval(uh)
    start = 0
    for tokens, rsl, csl in rims:
        n = tokens.shape[0]
        for ref, v in ((u_ext, uh), (k_ext, kvh[:, 0:C]), (v_ext, kvh[:, C:])):
            piece = v[start : start + n]
            piece = piece.reshape(3, CL, C) if csl is inside else unpacked(piece)
            ref[rsl, csl, :] = piece[0 : rsl.stop - rsl.start]
        start += n

    edge = [(3, RL - 6, 0, 8), (3, RL - 6, CL - 8, 8)]
    for col0 in range(0, CL, STRIP):
        edge += [(0, 3, col0, STRIP), (RL - 3, 3, col0, STRIP)]
    blocks(edge[0:5])
    blocks(edge[5:10])

    attended = att[...].reshape(RL * CL, C).astype(BF16)
    d_query = (dq[...] * 0.125).reshape(RL * CL, C).astype(BF16)
    cot_rows = cot[...].reshape(RL * CL, C)
    u = u_ext[...].reshape(RE * CE, C).astype(BF16)
    d_kv = jnp.concatenate(
        [dk_ext[...].reshape(RE * CE, C).astype(BF16), dv_ext[...].reshape(RE * CE, C).astype(BF16)], axis=-1
    )
    g_kv = dot(u, d_kv, TN)
    gsum[0:C, :] = dot(unit.astype(BF16), d_query, TN)
    gsum[C : 2 * C, :] = g_kv[:, 0:C]
    gsum[2 * C : 3 * C, :] = g_kv[:, C : 2 * C]
    gsum[3 * C : 4 * C, :] = dot(attended, cot_rows, TN)
    g16[...] = gsum[...].astype(BF16)
    bases = [lax.rem(y + d, yn) * gyn for d in range(yn)]
    for i, (dy, dc) in enumerate(plane):
        m = bases[dy] + cs[dc]
        pltpu.make_async_remote_copy(
            g16.at[pl.ds(pl.multiple_of(m * rows, rows), rows)],
            rs_rx.at[pl.ds(i * rows, rows)],
            a_send.at[0], a_recv.at[0], device_id=(ys[dy], cs[dc]), device_id_type=MESH,
        ).start()

    dn_ext[...] = dot(d_kv, wqkv[:, C : 3 * C], NT).reshape(RE, CE, C)
    for i, rsl in enumerate((above, below)):
        tx2_rows[i] = dn_ext[rsl, 4 : CL + 4, :].astype(BF16)
        for k, csl in enumerate((far_left, far_right)):
            tx2_corner[2 * i + k] = packed(dn_ext[rsl, csl, :])
    for k, csl in enumerate((far_left, far_right)):
        tx2_cols[k] = packed(dn_ext[level, csl, :])
    back = []
    for i, (dr, dc) in enumerate(around):
        if dc == 0:
            src, dst = tx2_rows.at[place(dr, 0) // 2], rx2_rows.at[place(dr, 0) // 2]
        elif dr == 0:
            src, dst = tx2_cols.at[place(0, dc)], rx2_cols.at[place(0, dc)]
        else:
            src, dst = tx2_corner.at[place(dr, dc)], rx2_corner.at[place(dr, dc)]
        copy = pltpu.make_async_remote_copy(
            src, dst, d_send.at[i], d_recv.at[i], device_id=beside(dr, dc), device_id_type=MESH
        )
        copy.start()
        back.append(copy)

    x = tok[...].astype(F32).reshape(RL * CL, C)
    out[...] = (x + dot(attended, wout[...])).astype(BF16).reshape(RL, CL, C)
    here = pl.ds(pl.multiple_of(me * rows, rows), rows)
    writes = [
        pltpu.make_async_copy(src, dst, out_sem.at[i])
        for i, (src, dst) in enumerate(
            ((out, out_hbm), (tgrad, tgrad_hbm), (own, summed_hbm.at[here]))
        )
    ]
    writes[0].start()
    for copy, _, to, _ in halo:
        pl.when(to)(copy.wait_send)

    wait_bytes(rs_rx, a_recv.at[0])
    mine = gsum[pl.ds(pl.multiple_of(me * rows, rows), rows), :]
    parts = rs_rx[...].astype(F32).reshape(na - 1, rows, C)
    z_rx[pl.ds(z, 1)] = (mine + jnp.sum(parts, axis=0)).astype(BF16)[None]
    for d in column:
        pltpu.make_async_remote_copy(
            z_rx.at[z], z_rx.at[z],
            a_send.at[1], a_recv.at[1], device_id=(zs[d], gy), device_id_type=MESH,
        ).start()

    for copy in back:
        copy.wait()
    first, last = slice(3, 6), slice(RL, RL + 3)
    left, right = slice(4, 8), slice(CL, CL + 4)
    dn_ext[last, inside, :] += rx2_rows[0].astype(F32)
    dn_ext[first, inside, :] += rx2_rows[1].astype(F32)
    dn_ext[level, right, :] += unpacked(rx2_cols[0].astype(F32))
    dn_ext[level, left, :] += unpacked(rx2_cols[1].astype(F32))
    for n, (rsl, csl) in enumerate(((last, right), (last, left), (first, right), (first, left))):
        dn_ext[rsl, csl, :] += unpacked(rx2_corner[n].astype(F32))[0:3]
    d_normed = dot(d_query, wqkv[:, 0:C], NT) + dn_ext[3 : RL + 3, 4 : CL + 4, :].reshape(RL * CL, C)
    x = tok[...].astype(F32).reshape(RL * CL, C)
    r = inverse_rms(x)
    unit = x * r
    g = d_normed * gains
    mean = jnp.sum(g * unit, axis=-1, keepdims=True) * (1.0 / C)
    grads = cot_rows.astype(F32) + r * (g - unit * mean)
    tgrad[...] = grads.astype(BF16).reshape(RL, CL, C)
    writes[1].start()

    wait_bytes(z_rx.at[pl.ds(0, zn - 1)], a_recv.at[1])
    own[...] = jnp.sum(z_rx[...].astype(F32), axis=0).astype(BF16)
    for dy, dc in plane:
        pltpu.make_async_remote_copy(
            own, summed_hbm.at[here],
            a_send.at[2], a_recv.at[2], device_id=(ys[dy], cs[dc]), device_id_type=MESH,
        ).start()
    writes[2].start()
    wait_bytes(z_rx.at[pl.ds(0, zn - 1)], a_send.at[1])
    wait_bytes(rs_rx, a_send.at[0])
    for write in writes:
        write.wait()
    wait_bytes(rs_rx, a_recv.at[2])
    wait_bytes(rs_rx, a_send.at[2])


def finish(
    factor, out, tgrad, summed, gain, wqkv, out_hbm, tgrad_hbm, qkvg_hbm, outg_hbm, gaing_hbm,
    out_v, tgrad_v, summed_v, gain_v, wqkv_v, qkvg, outg, gaing, r_sem, w_sem,
):
    held = ((summed, summed_v), (gain, gain_v), (wqkv, wqkv_v), (out, out_v), (tgrad, tgrad_v))
    reads = [pltpu.make_async_copy(src, dst, r_sem.at[i]) for i, (src, dst) in enumerate(held)]
    made = ((qkvg, qkvg_hbm), (outg, outg_hbm), (gaing, gaing_hbm), (out_v, out_hbm), (tgrad_v, tgrad_hbm))
    writes = [pltpu.make_async_copy(src, dst, w_sem.at[i]) for i, (src, dst) in enumerate(made)]
    for read in reads:
        read.start()
    eye = lax.broadcasted_iota(jnp.int32, (C, C), 0) == lax.broadcasted_iota(jnp.int32, (C, C), 1)
    reads[1].wait()
    gain_col = jnp.sum(jnp.where(eye, gain_v[...], 0.0), axis=1, keepdims=True) * factor
    reads[0].wait()
    reads[2].wait()
    outg[...] = summed_v[3 * C : 4 * C, :].astype(F32) * factor
    writes[1].start()
    total = jnp.zeros((C, C), F32)
    for i in range(3):
        piece = summed_v[i * C : (i + 1) * C, :].astype(F32)
        qkvg[:, i * C : (i + 1) * C] = piece * gain_col
        total += piece * wqkv_v[:, i * C : (i + 1) * C].astype(F32)
    writes[0].start()
    for i in (3, 4):
        reads[i].wait()
        writes[i].start()
    gain_sum = jnp.sum(total, axis=1, keepdims=True) * factor
    gaing[...] = jnp.sum(jnp.where(eye, gain_sum, 0.0), axis=0, keepdims=True)
    writes[2].start()
    for write in writes:
        write.wait()


def per_device(gxn, gyn, zn, tokens, norm_gain, qkv_weight, output_weight, cotangent):
    na = (gxn // zn) * gyn
    rows = 512 // na
    gain_row = norm_gain.reshape(1, C)
    hbm = pl.BlockSpec(memory_space=pl.ANY)
    images = (jax.ShapeDtypeStruct((RL, CL, C), BF16),) * 2
    results = images + (
        jax.ShapeDtypeStruct((C, 3 * C), F32),
        jax.ShapeDtypeStruct((C, C), F32),
        jax.ShapeDtypeStruct((1, C), F32),
    )
    image = pltpu.VMEM((RL, CL, C), BF16)
    image32 = pltpu.VMEM((RL, CL, C), F32)
    ext32 = pltpu.VMEM((RE, CE, C), F32)
    dma = pltpu.SemaphoreType.DMA
    cols = pltpu.VMEM((2, RL * 4, C), BF16)
    corners = pltpu.VMEM((4, 16, C), BF16)
    raw = pl.pallas_call(
        functools.partial(kernel, gxn, gyn, zn),
        out_shape=images + (jax.ShapeDtypeStruct((4 * C, C), BF16),),
        in_specs=[hbm] * 5,
        out_specs=(hbm,) * 3,
        scratch_shapes=[
            image,
            pltpu.VMEM((1, C), F32),
            pltpu.VMEM((C, 3 * C), BF16),
            pltpu.VMEM((C, C), BF16),
            image,
            image,
            image,
            cols,
            corners,
            pltpu.VMEM((2, 3, CL, C), BF16),
            cols,
            corners,
            ext32, ext32, ext32, ext32, ext32, ext32,
            image32, image32, image32, image32,
            pltpu.VMEM((2, 3, CL, C), BF16),
            cols,
            corners,
            pltpu.VMEM((2, 3, CL, C), BF16),
            cols,
            corners,
            pltpu.VMEM((4 * C, C), F32),
            pltpu.VMEM((4 * C, C), BF16),
            pltpu.VMEM(((na - 1) * rows, C), BF16),
            pltpu.VMEM((zn, rows, C), BF16),
            pltpu.VMEM((rows, C), BF16),
            dma((5,)), dma((3,)), dma((8,)), dma((8,)), dma((8,)), dma((8,)), dma((3,)), dma((3,)),
        ],
        compiler_params=pltpu.CompilerParams(
            collective_id=0, has_side_effects=True, vmem_limit_bytes=60 << 20
        ),
    )(
        tokens.reshape(RL, CL, C),
        gain_row,
        qkv_weight,
        output_weight,
        cotangent.reshape(RL, CL, C),
    )
    out, tgrad, qkvg, outg, gaing = pl.pallas_call(
        functools.partial(finish, (gxn * RL * gyn * CL) ** (-0.5)),
        out_shape=results,
        in_specs=[hbm] * 5,
        out_specs=(hbm,) * 5,
        scratch_shapes=[
            image,
            image,
            pltpu.VMEM((4 * C, C), BF16),
            pltpu.VMEM((1, C), F32),
            pltpu.VMEM((C, 3 * C), BF16),
            pltpu.VMEM((C, 3 * C), F32),
            pltpu.VMEM((C, C), F32),
            pltpu.VMEM((1, C), F32),
            dma((5,)),
            dma((5,)),
        ],
        compiler_params=pltpu.CompilerParams(vmem_limit_bytes=60 << 20),
    )(*raw, gain_row, qkv_weight)
    return (
        out.reshape(tokens.shape),
        tgrad.reshape(tokens.shape),
        qkvg,
        outg,
        gaing.reshape(C),
    )


def solution(mesh):
    gxn, gyn = mesh.shape["gx"], mesh.shape["gy"]
    image = P(None, "gx", "gy", None)
    return jax.shard_map(
        functools.partial(per_device, gxn, gyn, min(ZN, max(gxn // 4, 2))),
        mesh=mesh,
        in_specs=(image, P(), P(), P(), image),
        out_specs=(image, image, P(), P(), P()),
        check_vma=False,
    )
```

```python
import functools

import jax
import jax.numpy as jnp
from jax import lax
from jax.experimental import pallas as pl
from jax.experimental.pallas import tpu as pltpu
from jax.sharding import PartitionSpec as P

MESH = pl.DeviceIdType.MESH
EPS = 1e-06
F32 = jnp.float32
BF16 = jnp.bfloat16
C = 128
RL, CL = 16, 64
RE, CE = RL + 6, CL + 8
NB = CL // 8
STRIP = 16
NEG = -1e30
ZN = 8

NT = (((1,), (1,)), ((), ()))
TN = (((0,), (0,)), ((), ()))


def dot(a, b, dims=(((1,), (0,)), ((), ()))):
    return lax.dot_general(a, b, dims, preferred_element_type=F32)


def inverse_rms(x):
    return lax.rsqrt(jnp.sum(x * x, axis=-1, keepdims=True) * (1.0 / C) + EPS)


def kernel(
    gxn, gyn, zn,
    tok_hbm, gain_hbm, wqkv_hbm, wout_hbm, cot_hbm,
    out_hbm, tgrad_hbm, summed_hbm,
    tok, gain, wqkv, wout, cot,
    out, tgrad,
    tx_cols, tx_corner, rx_rows, rx_cols, rx_corner,
    u_ext, k_ext, v_ext, dk_ext, dv_ext, dn_ext,
    q_loc, da_loc, att, dq,
    tx2_rows, tx2_cols, tx2_corner, rx2_rows, rx2_cols, rx2_corner,
    unit_t, u_t, gsum, g16, rs_rx, z_rx, own,
    in_sem, out_sem, h_send, h_recv, d_send, d_recv, a_send, a_recv,
):
    yn = gxn // zn
    na = yn * gyn
    rows = 512 // na
    gx = lax.axis_index("gx")
    gy = lax.axis_index("gy")
    y, z = lax.div(gx, zn), lax.rem(gx, zn)
    me = y * gyn + gy
    ys = [lax.rem(y + d, yn) * zn + z for d in range(yn)]
    cs = [lax.rem(gy + d, gyn) for d in range(gyn)]
    zs = [y * zn + lax.rem(z + d, zn) for d in range(zn)]

    def far(d, n):
        return min(d, n - d)

    plane = sorted(
        ((dy, dc) for dy in range(yn) for dc in range(gyn) if dy or dc),
        key=lambda o: (-far(o[0], yn) - far(o[1], gyn) / 2, o),
    )
    column = sorted(range(1, zn), key=lambda d: (-far(d, zn), d))

    def beside(dr, dc):
        return (lax.rem(gx + (dr + gxn), gxn) if dr else gx, cs[dc % gyn])

    def exists(dr, dc):
        r, c = gx + dr, gy + dc
        return (r >= 0) & (r < gxn) & (c >= 0) & (c < gyn)

    def wait_bytes(ref, sem):
        pltpu.make_async_copy(ref, ref, sem).wait()

    fetches = [
        pltpu.make_async_copy(src, dst, in_sem.at[i])
        for i, (src, dst) in enumerate(
            ((tok_hbm, tok), (gain_hbm, gain), (wqkv_hbm, wqkv), (cot_hbm, cot), (wout_hbm, wout))
        )
    ]
    around = [(-1, 0), (1, 0), (-1, -1), (-1, 1), (1, -1), (1, 1), (0, -1), (0, 1)]
    barrier = pltpu.get_barrier_semaphore()

    def greet(device):
        pl.semaphore_signal(barrier, inc=1, device_id=device, device_id_type=MESH)

    for fetch in fetches:
        fetch.start()
    for d in column:
        greet((zs[d], gy))
    for dy, dc in plane:
        greet((ys[dy], cs[dc]))
    for dr, dc in around:
        if dr:
            greet(beside(dr, dc))
    fetches[0].wait()
    def packed(v):
        if v.shape[0] == 3:
            v = jnp.concatenate([v, v[0:1]], axis=0)
        half = v.shape[0] // 2
        return jnp.concatenate([v[0:half], v[half:]], axis=1).reshape(half * 8, C).astype(BF16)

    def unpacked(v):
        v = v.reshape(-1, 8, C)
        return jnp.concatenate([v[:, 0:4], v[:, 4:8]], axis=0)

    for k, csl in enumerate((slice(0, 4), slice(CL - 4, CL))):
        for n, rsl in enumerate((slice(0, 3), slice(RL - 3, RL))):
            tx_corner[2 * n + k] = packed(tok[rsl].astype(F32)[:, csl])
        tx_cols[k] = packed(tok[...].astype(F32)[:, csl])

    pl.semaphore_wait(barrier, 6 + (zn - 1) + (na - 1))

    def place(dr, dc):
        return 2 * (dr > 0) + (dc > 0)

    halo = []
    for i, (dr, dc) in enumerate(around):
        if dc == 0:
            src, dst = tok.at[slice(0, 3) if dr < 0 else slice(RL - 3, RL)], rx_rows.at[place(dr, 0) // 2]
        elif dr == 0:
            src, dst = tx_cols.at[place(0, dc)], rx_cols.at[place(0, dc)]
        else:
            src, dst = tx_corner.at[place(dr, dc)], rx_corner.at[place(dr, dc)]
        copy = pltpu.make_async_remote_copy(
            src, dst, h_send.at[i], h_recv.at[i], device_id=beside(dr, dc), device_id_type=MESH
        )
        halo.append((copy, dst, exists(dr, dc), exists(-dr, -dc)))
    for copy, _, to, _ in halo:
        pl.when(to)(copy.start)

    for fetch in fetches[1:]:
        fetch.wait()
    dk_ext[...] = jnp.zeros_like(dk_ext)
    dv_ext[...] = jnp.zeros_like(dv_ext)
    u_ext[...] = jnp.zeros_like(u_ext)
    gains = gain[...]

    def keyval(unit):
        return dot((unit * gains).astype(BF16), wqkv[:, C : 3 * C])

    x = tok[...].astype(F32).reshape(RL * CL, C)
    unit = x * inverse_rms(x)
    normed = (unit * gains).astype(BF16)
    u_ext[3 : RL + 3, 4 : CL + 4, :] = unit.reshape(RL, CL, C)
    unit_t[...] = unit.T.astype(BF16)
    projected = dot(normed, wqkv[...])
    q_loc[...] = (projected[:, 0:C] * 0.125).reshape(RL, CL, C)
    k_ext[3 : RL + 3, 4 : CL + 4, :] = projected[:, C : 2 * C].reshape(RL, CL, C)
    v_ext[3 : RL + 3, 4 : CL + 4, :] = projected[:, 2 * C : 3 * C].reshape(RL, CL, C)
    da_loc[...] = dot(cot[...].reshape(RL * CL, C), wout[...], NT).reshape(RL, CL, C)

    head0 = lax.broadcasted_iota(jnp.int32, (1, C), 1) < 64

    def two_heads(v):
        v = v.astype(BF16)
        zero = jnp.zeros_like(v)
        return jnp.concatenate([jnp.where(head0, v, zero), jnp.where(head0, zero, v)], axis=0)

    def blocks(places):
        each = []
        for row0, nr, col0, nc in places:
            kr, kc, nq = nr + 6, nc + 8, nr * nc
            keys = (slice(row0, row0 + kr), slice(col0, col0 + kc))
            own_at = (slice(row0, row0 + nr), slice(col0, col0 + nc))
            each.append((row0, nr, col0, nc, kr, kc, nq, keys, own_at))
        kws = [k_ext[b[7][0], b[7][1], :].reshape(b[4] * b[5], C).astype(BF16) for b in each]
        vws = [v_ext[b[7][0], b[7][1], :].reshape(b[4] * b[5], C).astype(BF16) for b in each]
        qbs = [two_heads(q_loc[b[8][0], b[8][1], :].reshape(b[6], C)) for b in each]
        dbs = [two_heads(da_loc[b[8][0], b[8][1], :].reshape(b[6], C)) for b in each]
        scores = [dot(kw, qb, NT) for kw, qb in zip(kws, qbs)]
        d_shares = [dot(vw, db, NT) for vw, db in zip(vws, dbs)]
        shares, lows = [], []
        for (row0, nr, col0, nc, kr, kc, nq, _, _), score in zip(each, scores):
            lanes = 2 * nq
            at = lax.broadcasted_iota(jnp.int32, (1, 1, lanes), 2) % nq
            q_row, q_col = at // nc, at % nc
            key_row = lax.broadcasted_iota(jnp.int32, (kr, 1, lanes), 0)
            key_col = lax.broadcasted_iota(jnp.int32, (1, kc, lanes), 1)
            image_row = gx * RL + row0 - 3 + key_row
            image_col = gy * CL + col0 - 4 + key_col
            row_bias = jnp.where(
                (key_row >= q_row) & (key_row <= q_row + 6) & (image_row >= 0) & (image_row < gxn * RL), 0.0, NEG
            )
            col_bias = jnp.where(
                (key_col >= q_col + 1) & (key_col <= q_col + 7) & (image_col >= 0) & (image_col < gyn * CL), 0.0, NEG
            )
            weights = jnp.exp(score.reshape(kr, kc, lanes) + row_bias + col_bias).reshape(kr * kc, lanes)
            totals = jnp.sum(weights, axis=0, keepdims=True)
            scale = jnp.where(totals > 1.0, 2.0**-64, 1.0)
            shares.append(weights * (1.0 / (totals * scale)) * scale)
            lows.append(shares[-1].astype(BF16))
        a2s = [dot(low, vw, TN) for low, vw in zip(lows, vws)]
        dvs = [dot(low, db) for low, db in zip(lows, dbs)]
        d_scores = []
        for share, d_share in zip(shares, d_shares):
            delta = jnp.sum(share * d_share, axis=0, keepdims=True)
            d_scores.append((share * (d_share - delta)).astype(BF16))
        dq2s = [dot(ds, kw, TN) for ds, kw in zip(d_scores, kws)]
        dks = [dot(ds, qb) for ds, qb in zip(d_scores, qbs)]
        for b, a2, dq2, dk, dv in zip(each, a2s, dq2s, dks, dvs):
            _, nr, _, nc, kr, kc, nq, keys, own_at = b
            att[own_at[0], own_at[1], :] = jnp.where(head0, a2[0:nq], a2[nq:]).reshape(nr, nc, C)
            dq[own_at[0], own_at[1], :] = jnp.where(head0, dq2[0:nq], dq2[nq:]).reshape(nr, nc, C)
            dk_ext[keys[0], keys[1], :] += dk.reshape(kr, kc, C)
            dv_ext[keys[0], keys[1], :] += dv.reshape(kr, kc, C)

    for j in range(1, NB - 1, 2):
        blocks([(3, RL - 6, j * 8, 8), (3, RL - 6, j * 8 + 8, 8)])


    above, below = slice(0, 3), slice(RL + 3, RE)
    level, far_left, far_right = slice(3, RL + 3), slice(0, 4), slice(CL + 4, CE)
    inside = slice(4, CL + 4)
    rims = (
        (rx_rows, 1, above, inside),
        (rx_rows, 0, below, inside),
        (rx_cols, 1, level, far_left),
        (rx_cols, 0, level, far_right),
        (rx_corner, 3, above, far_left),
        (rx_corner, 2, above, far_right),
        (rx_corner, 1, below, far_left),
        (rx_corner, 0, below, far_right),
    )
    has = ((-1, 0), (1, 0), (0, -1), (0, 1), (-1, -1), (-1, 1), (1, -1), (1, 1))

    def fill(copies, wanted):
        for copy, _, _, come in copies:
            pl.when(come)(copy.wait_recv)
        some = [(rims[n][0][rims[n][1]].reshape(-1, C), *rims[n][2:], has[n]) for n in wanted]
        xh = jnp.concatenate(
            [jnp.where(exists(*at), v.astype(F32), 0.0) for v, _, _, at in some], axis=0
        )
        uh = xh * inverse_rms(xh)
        kvh = keyval(uh)
        start = 0
        for tokens, rsl, csl, _ in some:
            n = tokens.shape[0]
            for ref, v in ((u_ext, uh), (k_ext, kvh[:, 0:C]), (v_ext, kvh[:, C:])):
                piece = v[start : start + n]
                piece = piece.reshape(3, CL, C) if csl is inside else unpacked(piece)
                ref[rsl, csl, :] = piece[0 : rsl.stop - rsl.start]
            start += n

    fill(halo[6:8], (2, 3))
    blocks([(3, RL - 6, 0, 8), (3, RL - 6, CL - 8, 8)])
    fill(halo[0:6], (0, 1, 4, 5, 6, 7))
    strips = [(row0, 3, col0, STRIP) for col0 in range(0, CL, STRIP) for row0 in (0, RL - 3)]
    u_t[...] = u_ext[...].reshape(RE * CE, C).T.astype(BF16)
    blocks(strips[0:4])
    blocks(strips[4:8])

    attended = att[...].reshape(RL * CL, C).astype(BF16)
    d_query = (dq[...] * 0.125).reshape(RL * CL, C).astype(BF16)
    cot_rows = cot[...].reshape(RL * CL, C)
    d_kv = jnp.concatenate(
        [dk_ext[...].reshape(RE * CE, C).astype(BF16), dv_ext[...].reshape(RE * CE, C).astype(BF16)], axis=-1
    )
    g_kv = dot(u_t[...], d_kv)
    gsum[0:C, :] = dot(unit_t[...], d_query)
    gsum[C : 2 * C, :] = g_kv[:, 0:C]
    gsum[2 * C : 3 * C, :] = g_kv[:, C : 2 * C]
    gsum[3 * C : 4 * C, :] = dot(attended, cot_rows, TN)
    g16[...] = gsum[...].astype(BF16)
    bases = [lax.rem(y + d, yn) * gyn for d in range(yn)]
    for i, (dy, dc) in enumerate(plane):
        m = bases[dy] + cs[dc]
        pltpu.make_async_remote_copy(
            g16.at[pl.ds(pl.multiple_of(m * rows, rows), rows)],
            rs_rx.at[pl.ds(i * rows, rows)],
            a_send.at[0], a_recv.at[0], device_id=(ys[dy], cs[dc]), device_id_type=MESH,
        ).start()

    dn_ext[...] = dot(d_kv, wqkv[:, C : 3 * C], NT).reshape(RE, CE, C)
    for i, rsl in enumerate((above, below)):
        tx2_rows[i] = dn_ext[rsl, 4 : CL + 4, :].astype(BF16)
        for k, csl in enumerate((far_left, far_right)):
            tx2_corner[2 * i + k] = packed(dn_ext[rsl, csl, :])
    for k, csl in enumerate((far_left, far_right)):
        tx2_cols[k] = packed(dn_ext[level, csl, :])
    back = []
    for i, (dr, dc) in enumerate(around):
        if dc == 0:
            src, dst = tx2_rows.at[place(dr, 0) // 2], rx2_rows.at[place(dr, 0) // 2]
        elif dr == 0:
            src, dst = tx2_cols.at[place(0, dc)], rx2_cols.at[place(0, dc)]
        else:
            src, dst = tx2_corner.at[place(dr, dc)], rx2_corner.at[place(dr, dc)]
        copy = pltpu.make_async_remote_copy(
            src, dst, d_send.at[i], d_recv.at[i], device_id=beside(dr, dc), device_id_type=MESH
        )
        copy.start()
        back.append(copy)

    x = tok[...].astype(F32).reshape(RL * CL, C)
    out[...] = (x + dot(attended, wout[...])).astype(BF16).reshape(RL, CL, C)
    here = pl.ds(pl.multiple_of(me * rows, rows), rows)
    writes = [
        pltpu.make_async_copy(src, dst, out_sem.at[i])
        for i, (src, dst) in enumerate(
            ((out, out_hbm), (tgrad, tgrad_hbm), (own, summed_hbm.at[here]))
        )
    ]
    writes[0].start()
    for copy, _, to, _ in halo:
        pl.when(to)(copy.wait_send)

    wait_bytes(rs_rx, a_recv.at[0])
    mine = gsum[pl.ds(pl.multiple_of(me * rows, rows), rows), :]
    parts = rs_rx[...].astype(F32).reshape(na - 1, rows, C)
    z_rx[pl.ds(z, 1)] = (mine + jnp.sum(parts, axis=0)).astype(BF16)[None]
    for d in column:
        pltpu.make_async_remote_copy(
            z_rx.at[z], z_rx.at[z],
            a_send.at[1], a_recv.at[1], device_id=(zs[d], gy), device_id_type=MESH,
        ).start()

    for copy in back:
        copy.wait()
    first, last = slice(3, 6), slice(RL, RL + 3)
    left, right = slice(4, 8), slice(CL, CL + 4)
    dn_ext[last, inside, :] += rx2_rows[0].astype(F32)
    dn_ext[first, inside, :] += rx2_rows[1].astype(F32)
    dn_ext[level, right, :] += unpacked(rx2_cols[0].astype(F32))
    dn_ext[level, left, :] += unpacked(rx2_cols[1].astype(F32))
    for n, (rsl, csl) in enumerate(((last, right), (last, left), (first, right), (first, left))):
        dn_ext[rsl, csl, :] += unpacked(rx2_corner[n].astype(F32))[0:3]
    d_normed = dot(d_query, wqkv[:, 0:C], NT) + dn_ext[3 : RL + 3, 4 : CL + 4, :].reshape(RL * CL, C)
    x = tok[...].astype(F32).reshape(RL * CL, C)
    r = inverse_rms(x)
    unit = x * r
    g = d_normed * gains
    mean = jnp.sum(g * unit, axis=-1, keepdims=True) * (1.0 / C)
    grads = cot_rows.astype(F32) + r * (g - unit * mean)
    tgrad[...] = grads.astype(BF16).reshape(RL, CL, C)
    writes[1].start()

    wait_bytes(z_rx.at[pl.ds(0, zn - 1)], a_recv.at[1])
    own[...] = jnp.sum(z_rx[...].astype(F32), axis=0).astype(BF16)
    for dy, dc in plane:
        pltpu.make_async_remote_copy(
            own, summed_hbm.at[here],
            a_send.at[2], a_recv.at[2], device_id=(ys[dy], cs[dc]), device_id_type=MESH,
        ).start()
    writes[2].start()
    wait_bytes(z_rx.at[pl.ds(0, zn - 1)], a_send.at[1])
    wait_bytes(rs_rx, a_send.at[0])
    for write in writes:
        write.wait()
    wait_bytes(rs_rx, a_recv.at[2])
    wait_bytes(rs_rx, a_send.at[2])


def finish(
    factor, out, tgrad, summed, gain, wqkv, out_hbm, tgrad_hbm, qkvg_hbm, outg_hbm, gaing_hbm,
    out_v, tgrad_v, summed_v, gain_v, wqkv_v, qkvg, outg, gaing, r_sem, w_sem,
):
    held = ((summed, summed_v), (gain, gain_v), (wqkv, wqkv_v), (out, out_v), (tgrad, tgrad_v))
    reads = [pltpu.make_async_copy(src, dst, r_sem.at[i]) for i, (src, dst) in enumerate(held)]
    made = ((qkvg, qkvg_hbm), (outg, outg_hbm), (gaing, gaing_hbm), (out_v, out_hbm), (tgrad_v, tgrad_hbm))
    writes = [pltpu.make_async_copy(src, dst, w_sem.at[i]) for i, (src, dst) in enumerate(made)]
    for read in reads:
        read.start()
    eye = lax.broadcasted_iota(jnp.int32, (C, C), 0) == lax.broadcasted_iota(jnp.int32, (C, C), 1)
    reads[1].wait()
    gain_col = jnp.sum(jnp.where(eye, gain_v[...], 0.0), axis=1, keepdims=True) * factor
    reads[0].wait()
    reads[2].wait()
    outg[...] = summed_v[3 * C : 4 * C, :].astype(F32) * factor
    writes[1].start()
    total = jnp.zeros((C, C), F32)
    for i in range(3):
        piece = summed_v[i * C : (i + 1) * C, :].astype(F32)
        qkvg[:, i * C : (i + 1) * C] = piece * gain_col
        total += piece * wqkv_v[:, i * C : (i + 1) * C].astype(F32)
    writes[0].start()
    for i in (3, 4):
        reads[i].wait()
        writes[i].start()
    gain_sum = jnp.sum(total, axis=1, keepdims=True) * factor
    gaing[...] = jnp.sum(jnp.where(eye, gain_sum, 0.0), axis=0, keepdims=True)
    writes[2].start()
    for write in writes:
        write.wait()


def per_device(gxn, gyn, zn, tokens, norm_gain, qkv_weight, output_weight, cotangent):
    na = (gxn // zn) * gyn
    rows = 512 // na
    gain_row = norm_gain.reshape(1, C)
    hbm = pl.BlockSpec(memory_space=pl.ANY)
    images = (jax.ShapeDtypeStruct((RL, CL, C), BF16),) * 2
    results = images + (
        jax.ShapeDtypeStruct((C, 3 * C), F32),
        jax.ShapeDtypeStruct((C, C), F32),
        jax.ShapeDtypeStruct((1, C), F32),
    )
    image = pltpu.VMEM((RL, CL, C), BF16)
    image32 = pltpu.VMEM((RL, CL, C), F32)
    ext32 = pltpu.VMEM((RE, CE, C), F32)
    dma = pltpu.SemaphoreType.DMA
    cols = pltpu.VMEM((2, RL * 4, C), BF16)
    corners = pltpu.VMEM((4, 16, C), BF16)
    raw = pl.pallas_call(
        functools.partial(kernel, gxn, gyn, zn),
        out_shape=images + (jax.ShapeDtypeStruct((4 * C, C), BF16),),
        in_specs=[hbm] * 5,
        out_specs=(hbm,) * 3,
        scratch_shapes=[
            image,
            pltpu.VMEM((1, C), F32),
            pltpu.VMEM((C, 3 * C), BF16),
            pltpu.VMEM((C, C), BF16),
            image,
            image,
            image,
            cols,
            corners,
            pltpu.VMEM((2, 3, CL, C), BF16),
            cols,
            corners,
            ext32, ext32, ext32, ext32, ext32, ext32,
            image32, image32, image32, image32,
            pltpu.VMEM((2, 3, CL, C), BF16),
            cols,
            corners,
            pltpu.VMEM((2, 3, CL, C), BF16),
            cols,
            corners,
            pltpu.VMEM((C, RL * CL), BF16),
            pltpu.VMEM((C, RE * CE), BF16),
            pltpu.VMEM((4 * C, C), F32),
            pltpu.VMEM((4 * C, C), BF16),
            pltpu.VMEM(((na - 1) * rows, C), BF16),
            pltpu.VMEM((zn, rows, C), BF16),
            pltpu.VMEM((rows, C), BF16),
            dma((5,)), dma((3,)), dma((8,)), dma((8,)), dma((8,)), dma((8,)), dma((3,)), dma((3,)),
        ],
        compiler_params=pltpu.CompilerParams(
            collective_id=0, has_side_effects=True, vmem_limit_bytes=60 << 20
        ),
    )(
        tokens.reshape(RL, CL, C),
        gain_row,
        qkv_weight,
        output_weight,
        cotangent.reshape(RL, CL, C),
    )
    out, tgrad, qkvg, outg, gaing = pl.pallas_call(
        functools.partial(finish, (gxn * RL * gyn * CL) ** (-0.5)),
        out_shape=results,
        in_specs=[hbm] * 5,
        out_specs=(hbm,) * 5,
        scratch_shapes=[
            image,
            image,
            pltpu.VMEM((4 * C, C), BF16),
            pltpu.VMEM((1, C), F32),
            pltpu.VMEM((C, 3 * C), BF16),
            pltpu.VMEM((C, 3 * C), F32),
            pltpu.VMEM((C, C), F32),
            pltpu.VMEM((1, C), F32),
            dma((5,)),
            dma((5,)),
        ],
        compiler_params=pltpu.CompilerParams(vmem_limit_bytes=60 << 20),
    )(*raw, gain_row, qkv_weight)
    return (
        out.reshape(tokens.shape),
        tgrad.reshape(tokens.shape),
        qkvg,
        outg,
        gaing.reshape(C),
    )


def solution(mesh):
    gxn, gyn = mesh.shape["gx"], mesh.shape["gy"]
    image = P(None, "gx", "gy", None)
    return jax.shard_map(
        functools.partial(per_device, gxn, gyn, min(ZN, max(gxn // 4, 2))),
        mesh=mesh,
        in_specs=(image, P(), P(), P(), image),
        out_specs=(image, image, P(), P(), P()),
        check_vma=False,
    )
```
